512 devices in a mesh: chan: 64 (over x_hi, z, core), tm: 8 (over x_lo, y).
Axes of the slice: x: 4 (x_hi: 2, x_lo: 2; x = x_hi * 2 + x_lo), y: 4, z: 16, core: 2. Of those that a mesh axis runs over, the one named last changes fastest.
Arguments:
- traces: bfloat16 [6144, 65536], P('chan', 'tm'), may hold values from -6 to 6
- live_channels: int32 [64], P('chan'), may hold values from 48 to 96
- partners: int32 [64, 3], P('chan'), may hold values from -1 to 63, as said below
Outputs:
- lags: float32 [6144, 3, 1024], P('chan', None, 'tm')
The draws below stay inside these ranges and needn't reach their ends.
Inputs may be any that keep to these rules, and one draw needn't show every extreme that they name: `partners`: row a lists distinct blocks b with a < b <= a + 3 and b < 64, ascending, then -1 in the empty slots. Block 0 lists all 3; the last block lists none.
All inputs are finite; a program needn't handle non-finite values.
Results may differ from the reference program's by a relative error of at most 0.0064.
Values may be sent and summed in bfloat16 or wider, within the bound.
A program may use at most 128 MiB of HBM per device.

```python
import math
import jax
import jax.numpy as jnp
from jax import lax

CB = 96
NFFT = 1024
SMOOTH = 64
LIMIT = 3
BLOCKS = 64
CHANNELS = 6144
SEGMENTS = 128
SAMPLES = 65536


def draw_partners(key, part):
    key = jax.random.fold_in(key, 7)
    picked = jax.random.randint(key, (BLOCKS, LIMIT), 0, 10) < 6
    rows = jnp.arange(BLOCKS, dtype=jnp.int32)[:, None]
    offsets = jnp.arange(1, LIMIT + 1, dtype=jnp.int32)[None, :]
    picked = picked | (rows == 0) | (rows == BLOCKS - 2) & (offsets == 1)
    target = rows + offsets
    keep = picked & (target < BLOCKS)
    values = jnp.sort(jnp.where(keep, target, BLOCKS + LIMIT + 1), axis=1)
    return jnp.where(values >= BLOCKS, -1, values).astype(jnp.int32)


def touch_ends(entries, rng, least, high):
    shape = entries.shape
    index_at = [jax.random.randint(jax.random.fold_in(rng, axis), (), 0, shape[axis]) for axis in range(len(shape))]
    entries = entries.at[tuple(index_at)].set(least)
    longest = shape.index(max(shape))
    index_at[longest] = (index_at[longest] + 1) % shape[longest]
    return entries.at[tuple(index_at)].set(high)


def block_scale(rng, dims, shards, least, largest):
    def one(dim, blocks):
        draws = jax.random.uniform(jax.random.fold_in(jax.random.fold_in(rng, 6), dim), (blocks,), jnp.float32, least / len(shards), largest / len(shards))
        return jnp.repeat(jnp.exp(draws), dims[dim] // blocks).reshape((-1,) + (1,) * (len(dims) - dim - 1))

    gain = one(*shards[0])
    for cut in shards[1:]:
        gain = gain * one(*cut)
    return gain


def scatter_about(stream_key, extent, width, most, shards=(), kind=jnp.bfloat16):
    drawn = jax.random.normal(stream_key, extent, jnp.float32) * width
    if len(shards) > 0:
        drawn = block_scale(stream_key, extent, shards, -0.22, 0.18) * drawn
    return jnp.clip(drawn, min=-most, max=most).astype(kind)


def setup_inputs(seed: int = 0) -> dict:
    keys = jax.random.split(jax.random.key(seed), 4)
    traces = scatter_about(keys[0], (CHANNELS, SAMPLES), 1.0, 6.0, ((0, 64), (1, 8)))
    live_channels = touch_ends(jax.random.randint(keys[1], (BLOCKS,), CB // 2, CB + 1), jax.random.fold_in(keys[1], 1), CB // 2, CB).astype(jnp.int32)
    partners = draw_partners(jax.random.fold_in(keys[3], 71), 0)
    return dict(traces=traces, live_channels=live_channels, partners=partners)


def hann_taper(length):
    steps = jnp.arange(length, dtype=jnp.float32)
    return 0.5 - 0.5 * jnp.cos(steps * (2.0 * math.pi / length))

def forward_table(length):
    half = length // 2
    samples = jnp.arange(length, dtype=jnp.int32)[:, None]
    freqs = jnp.arange(1, half + 1, dtype=jnp.int32)[None, :]
    phase = (samples * freqs % length).astype(jnp.float32) * (2.0 * math.pi / length)
    return jnp.concatenate([jnp.cos(phase), -jnp.sin(phase)], 1).astype(jnp.bfloat16)

def band_matrix(half, window):
    source = jnp.arange(half, dtype=jnp.int32)[:, None]
    target = jnp.arange(half, dtype=jnp.int32)[None, :]
    start = jnp.clip(target - window // 2, 0, half - window)
    return ((source >= start) & (source < start + window)).astype(jnp.float32)

def lag_table(length, first, count):
    half = length // 2
    freqs = jnp.arange(1, half + 1, dtype=jnp.int32)[:, None]
    shifts = (first + jnp.arange(count, dtype=jnp.int32))[None, :]
    phase = (freqs * shifts % length).astype(jnp.float32) * (2.0 * math.pi / length)
    weight = jnp.where(freqs < half, 2.0, 1.0).astype(jnp.float32) / math.sqrt(length)
    return jnp.concatenate([weight * jnp.cos(phase), -weight * jnp.sin(phase)], 0)

def whiten(extended, length):
    hop = length // 2
    chans = extended.shape[0]
    segs = extended.shape[1] // hop - 1
    first = extended[:, :segs * hop].reshape(chans, segs, hop)
    second = extended[:, hop:].reshape(chans, segs, hop)
    pieces = jnp.concatenate([first, second], 2)
    tapered = (pieces.astype(jnp.float32) * hann_taper(length)).astype(jnp.bfloat16)
    spectra = jnp.dot(tapered.reshape(-1, length), forward_table(length), preferred_element_type=jnp.float32)
    real_part = spectra[:, :hop]
    imag_part = spectra[:, hop:]
    power = real_part * real_part + imag_part * imag_part
    smooth = jnp.dot(power, band_matrix(hop, SMOOTH), precision=lax.Precision.HIGHEST) / SMOOTH
    factor = lax.rsqrt(smooth + 1e-06)
    white = (spectra * jnp.concatenate([factor, factor], 1)).astype(jnp.bfloat16)
    return white.reshape(chans, segs, length)

def cross_stack(own, partner):
    hop = own.shape[2] // 2
    own_re = own[:, :, :hop].astype(jnp.float32)
    own_im = own[:, :, hop:].astype(jnp.float32)
    par_re = partner[:, :, :hop].astype(jnp.float32)
    par_im = partner[:, :, hop:].astype(jnp.float32)
    real_sum = lax.optimization_barrier(jnp.sum(own_re * par_re + own_im * par_im, axis=1))
    imag_sum = lax.optimization_barrier(jnp.sum(own_im * par_re - own_re * par_im, axis=1))
    return jnp.concatenate([real_sum, imag_sum], 1)

def reference(traces, live_channels, partners):
    length = NFFT
    hop = length // 2
    alive = jnp.arange(CHANNELS, dtype=jnp.int32) % CB < jnp.repeat(live_channels, CB)
    masked = jnp.where(alive[:, None], traces, jnp.zeros_like(traces))
    extended = jnp.concatenate([masked, jnp.zeros((CHANNELS, hop), jnp.bfloat16)], 1)
    white = lax.map(lambda block: whiten(block, length), extended.reshape(BLOCKS, CB, -1))
    table = lag_table(length, 0, length)

    def one_block(index):
        own = white[index]
        rows = []
        for slot in range(LIMIT):
            target = partners[index, slot]
            partner = lax.dynamic_index_in_dim(white, jnp.maximum(target, 0).astype(jnp.int32), 0, keepdims=False)
            rows.append(jnp.where(target >= 0, cross_stack(own, partner), jnp.float32(0.0)))
        mean = jnp.stack(rows, 1) / SEGMENTS
        return jnp.dot(mean.reshape(-1, length), table, precision=lax.Precision.HIGHEST).reshape(CB, LIMIT, length)
    result = lax.map(one_block, jnp.arange(BLOCKS, dtype=jnp.int32))
    return result.reshape(CHANNELS, LIMIT, length)
```

```python
import functools
import math

import jax
import jax.numpy as jnp
import ml_dtypes
import numpy as np
from jax import lax
from jax.experimental import pallas as pl
from jax.experimental.pallas import tpu as pltpu
from jax.sharding import PartitionSpec as P

NFFT = 1024
HOP = NFFT // 2
SMOOTH = 64
LIMIT = 3
MESH = pl.DeviceIdType.MESH
F32 = jnp.float32
BF16 = jnp.bfloat16

SLOT_A, SLOT_B, SLOT_C, SLOT_D, SLOT_E = range(5)
PAIRS = 6


def bin_order():
    return np.concatenate([np.arange(2, HOP + 1, 2), np.arange(1, HOP, 2)])


def taper_rows():
    steps = np.arange(NFFT, dtype=np.float64)
    return (0.5 - 0.5 * np.cos(steps * (2.0 * math.pi / NFFT))).astype(np.float32).reshape(2, HOP)


def forward_tables():
    samples = np.arange(HOP)[:, None]
    tables = []
    for bins in (bin_order()[None, : HOP // 2], bin_order()[None, HOP // 2 :]):
        phase = (samples * bins % NFFT) * (2.0 * math.pi / NFFT)
        tables.append(np.concatenate([np.cos(phase), -np.sin(phase)], 1))
    return np.stack(tables).astype(ml_dtypes.bfloat16)


def band_table():
    freqs = bin_order() - 1
    start = np.clip(freqs - SMOOTH // 2, 0, HOP - SMOOTH)[None, :]
    source = freqs[:, None]
    return (((source >= start) & (source < start + SMOOTH)) / SMOOTH).astype(ml_dtypes.bfloat16)


def lag_tables(segments):
    shifts = np.arange(HOP)[None, :]
    tables = []
    for bins in (bin_order()[: HOP // 2, None], bin_order()[HOP // 2 :, None]):
        phase = (bins * shifts % NFFT) * (2.0 * math.pi / NFFT)
        weight = np.where(bins < HOP, 2.0, 1.0) / math.sqrt(NFFT) / segments
        tables.append(np.concatenate([weight * np.cos(phase), -weight * np.sin(phase)], 0))
    return np.stack(tables).astype(ml_dtypes.bfloat16)


def chunk_bounds(segs):
    bounds = [(4 * s + 1, 4 * s + 5) for s in range(segs // 4)]
    bounds[0] = (0, 5)
    bounds[-1] = (bounds[-1][0], segs)
    return bounds


def kernel(
    nq, nt, segs, chans,
    live_hbm, partners_hbm, x_ref, taper_hbm, fwd_hbm, band_hbm, lag_hbm, out_ref,
    live, partners, taper, own, buf, white, acc, fwd, band, lagt, part, gath, fin, res,
    load_sem, table_sem, ssem, rsem, hsend, hrecv, asend, arecv, fsend, frecv,
):
    half = chans // 2
    steps = segs // 4
    cols = NFFT // nt
    chunks = chunk_bounds(segs)
    chan = lax.axis_index("chan")
    t = lax.axis_index("tm")
    q = chan // 2
    c = lax.rem(chan, 2)
    below, above = q > 0, q < nq - 1
    mine = SLOT_B + c
    theirs = SLOT_C - c

    def at(chip, core, time):
        return {"chan": 2 * chip + core, "tm": time}

    for h in range(segs):
        pltpu.make_async_copy(x_ref.at[:, pl.ds(HOP * h, HOP)], own.at[h], load_sem.at[h]).start()
    tables = [
        pltpu.make_async_copy(fwd_hbm, fwd, table_sem.at[0]),
        pltpu.make_async_copy(band_hbm, band, table_sem.at[1]),
        pltpu.make_async_copy(lag_hbm, lagt, table_sem.at[2]),
        pltpu.make_async_copy(taper_hbm, taper, table_sem.at[3]),
        pltpu.make_async_copy(partners_hbm, partners, table_sem.at[4]),
    ]
    live_copy = pltpu.make_async_copy(live_hbm, live, table_sem.at[5])
    live_copy.start()
    for copy in tables:
        copy.start()

    @pl.when(q == 0)
    def _():
        buf[SLOT_A] = jnp.zeros((segs + 1, half, HOP), BF16)

    @pl.when(q == nq - 1)
    def _():
        buf[SLOT_D] = jnp.zeros((segs + 1, half, HOP), BF16)
        buf[SLOT_E] = jnp.zeros((segs + 1, half, HOP), BF16)
        res[...] = jnp.zeros(res.shape, F32)

    @pl.when(t == nt - 1)
    def _():
        for slot in range(5):
            buf[slot, segs] = jnp.zeros((half, HOP), BF16)

    barrier = pltpu.get_barrier_semaphore()

    def greet(chip, core, time):
        pl.semaphore_signal(barrier, inc=1, device_id=at(chip, core, time), device_id_type=MESH)

    for d in range(1, nt):
        greet(q, c, lax.rem(t + d, nt))

    def greet_around(time):
        greet(q, 1 - c, time)

        @pl.when(below)
        def _():
            greet(q - 1, 0, time)
            greet(q - 1, 1, time)

        @pl.when(above)
        def _():
            greet(q + 1, 0, time)
            greet(q + 1, 1, time)

    greet_around(t)

    @pl.when(t > 0)
    def _():
        greet_around(t - 1)

    @pl.when(t < nt - 1)
    def _():
        greet_around(t + 1)

    live_copy.wait()
    alive = lax.broadcasted_iota(jnp.int32, (chans, HOP), 0) < live[0]
    mask = jnp.where(alive, F32(1.0), F32(0.0)).astype(BF16)

    def mask_one(h, carry):
        pltpu.make_async_copy(
            x_ref.at[:, pl.ds(pl.multiple_of(HOP * h, HOP), HOP)], own.at[h], load_sem.at[h]
        ).wait()
        own[h] = own[h] * mask
        buf[mine, h] = own[h, pl.ds(pl.multiple_of(half * c, half), half), :]
        return carry

    lax.fori_loop(0, segs, mask_one, 0)

    around = 1 + 2 * jnp.where(below, 1, 0) + 2 * jnp.where(above, 1, 0)
    times = 1 + jnp.where(t > 0, 1, 0) + jnp.where(t < nt - 1, 1, 0)
    pl.semaphore_wait(barrier, nt - 1 + around * times)

    outward = 2 * c - 1
    main_ok = jnp.where(c == 0, q, nq - 1 - q) > 0
    edge_ok = c * q > 0

    def route(index):
        if index == 0:
            return half * (1 - c), mine, q, 1 - c
        if index in (1, 2):
            return half * (index - 1), 3 * (1 - c), q + outward, index - 1
        if index in (3, 4):
            return half * (index - 3), SLOT_E, q - 1, index - 3
        return half * c, mine, q, c

    def stream(index, k):
        lo, hi = chunks[k]
        row, slot, chip, core = route(index)
        return pltpu.make_async_remote_copy(
            src_ref=own.at[pl.ds(lo, hi - lo), pl.ds(row, half), :],
            dst_ref=buf.at[slot, pl.ds(lo, hi - lo)],
            send_sem=ssem.at[index, k],
            recv_sem=rsem.at[slot, k],
            device_id=at(chip, core, t),
            device_id_type=MESH,
        )

    def halo(index):
        row, slot, chip, core = route(index)
        return pltpu.make_async_remote_copy(
            src_ref=own.at[0, pl.ds(row, half), :],
            dst_ref=buf.at[slot, segs],
            send_sem=hsend.at[index],
            recv_sem=hrecv.at[slot],
            device_id=at(chip, core, t - 1),
            device_id_type=MESH,
        )

    def halos(act):
        @pl.when(t > 0)
        def _():
            act(halo(5))
            act(halo(0))

            @pl.when(main_ok)
            def _():
                act(halo(1))
                act(halo(2))

            @pl.when(edge_ok)
            def _():
                act(halo(3))
                act(halo(4))

    def arrive(slot, k):
        lo, hi = chunks[k]
        pltpu.make_async_remote_copy(
            src_ref=own.at[pl.ds(lo, hi - lo), pl.ds(0, half), :],
            dst_ref=buf.at[slot, pl.ds(lo, hi - lo)],
            send_sem=ssem.at[0, k],
            recv_sem=rsem.at[slot, k],
            device_id=at(q, 1 - c, t),
            device_id_type=MESH,
        ).wait_recv()

    def halo_wait(slot):
        @pl.when(t < nt - 1)
        def _():
            pltpu.make_async_remote_copy(
                src_ref=own.at[0, pl.ds(0, half), :],
                dst_ref=buf.at[slot, segs],
                send_sem=hsend.at[0],
                recv_sem=hrecv.at[slot],
                device_id=at(q, c, t + 1),
                device_id_type=MESH,
            ).wait_recv()

    def main_start(k):
        @pl.when(main_ok)
        def _():
            stream(1, k).start()
            stream(2, k).start()

    def main_left(k):
        @pl.when(main_ok)
        def _():
            stream(1, k).wait_send()
            stream(2, k).wait_send()

    def edge_start(k):
        @pl.when(edge_ok)
        def _():
            stream(3, k).start()
            stream(4, k).start()

    stream(0, 0).start()
    main_start(0)
    halos(lambda copy: copy.start())
    for k in range(1, steps):
        stream(0, k).start()
    main_start(1)

    @pl.when(c == 1)
    def _():
        for k in range(2, steps):
            main_start(k)

    for copy in tables:
        copy.wait()

    taper_rise, taper_fall = taper[0:1, :], taper[1:2, :]
    quarter = HOP // 2

    def whiten(parts):
        sums, differences = [], []
        for slot, first, count in parts:
            samples = buf[slot, first : first + count + 1].astype(F32)
            rise, fall = samples[:count] * taper_rise, samples[1:] * taper_fall
            sums.append((rise + fall).astype(BF16).reshape(count * half, HOP))
            differences.append((rise - fall).astype(BF16).reshape(count * half, HOP))
        even = jnp.dot(jnp.concatenate(sums, 0), fwd[0], preferred_element_type=F32)
        odd = jnp.dot(jnp.concatenate(differences, 0), fwd[1], preferred_element_type=F32)
        power = [
            (z[:, :quarter] * z[:, :quarter] + z[:, quarter:] * z[:, quarter:]).astype(BF16)
            for z in (even, odd)
        ]
        smooth = jnp.dot(jnp.concatenate(power, 1), band[...], preferred_element_type=F32)
        factor = lax.rsqrt(smooth + 1e-06)
        row = 0
        for slot, first, count in parts:
            rows = slice(row, row + count * half)
            row += count * half
            for n, z in enumerate((even, odd)):
                scale = factor[rows, n * quarter : (n + 1) * quarter]
                for m in range(2):
                    value = (z[rows, m * quarter : (m + 1) * quarter] * scale).astype(BF16)
                    lanes = slice(m * HOP + n * quarter, m * HOP + (n + 1) * quarter)
                    white[slot, first : first + count, :, lanes] = value.reshape(count, half, quarter)

    def cross(pairs, start, count):
        slots = []
        for _, first, second in pairs:
            for slot in (first, second):
                if not any(slot is s for s in slots):
                    slots.append(slot)

        def tile(i, carry):
            rows = pl.ds(pl.multiple_of(16 * (i // 4), 16), 16)
            lanes = pl.multiple_of(128 * lax.rem(i, 4), 128)
            lanes_re, lanes_im = pl.ds(lanes, 128), pl.ds(HOP + lanes, 128)
            sums = [[acc[p, rows, lanes_re], acc[p, rows, lanes_im]] for p, _, _ in pairs]
            for seg in range(start, start + count):
                values = [
                    (
                        white[slot, seg, rows, lanes_re].astype(F32),
                        white[slot, seg, rows, lanes_im].astype(F32),
                    )
                    for slot in slots
                ]
                for n, (_, first, second) in enumerate(pairs):
                    a_re, a_im = [v for s, v in zip(slots, values) if s is first][0]
                    b_re, b_im = [v for s, v in zip(slots, values) if s is second][0]
                    sums[n][0] += a_re * b_re + a_im * b_im
                    sums[n][1] += a_im * b_re - a_re * b_im
            for n, (p, _, _) in enumerate(pairs):
                acc[p, rows, lanes_re] = sums[n][0]
                acc[p, rows, lanes_im] = sums[n][1]
            return carry

        lax.fori_loop(0, (half // 16) * 4, tile, 0)

    def lags_of(first, count):
        stack = acc[first : first + count].reshape(count * half, NFFT)
        high = stack.astype(BF16)
        low = (stack - high.astype(F32)).astype(BF16)
        both = jnp.concatenate([high, low], 0)
        sides = []
        for n in range(2):
            lanes = slice(n * quarter, (n + 1) * quarter)
            lanes_im = slice(HOP + n * quarter, HOP + (n + 1) * quarter)
            side = jnp.dot(
                jnp.concatenate([both[:, lanes], both[:, lanes_im]], 1),
                lagt[n],
                preferred_element_type=F32,
            )
            sides.append(side[: count * half] + side[count * half :])
        even, odd = sides
        lags = jnp.concatenate([(even + odd).astype(BF16), (even - odd).astype(BF16)], 1)
        for time in range(nt):
            part[time, first : first + count] = lags[:, time * cols : (time + 1) * cols].reshape(
                count, half, cols
            )

    def exchange(group, first, count, d):
        peer = lax.rem(t + d, nt)
        return pltpu.make_async_remote_copy(
            src_ref=part.at[peer, pl.ds(first, count)],
            dst_ref=gath.at[t, pl.ds(first, count)],
            send_sem=asend.at[group, d],
            recv_sem=arecv.at[group, t],
            device_id=at(q, c, peer),
            device_id_type=MESH,
        )

    def collect(group, first, count):
        gath[t, first : first + count] = part[t, first : first + count]
        for d in range(1, nt):
            source = lax.rem(t + d, nt)
            pltpu.make_async_remote_copy(
                src_ref=part.at[source, pl.ds(first, count)],
                dst_ref=gath.at[source, pl.ds(first, count)],
                send_sem=asend.at[group, d],
                recv_sem=arecv.at[group, source],
                device_id=at(q, c, source),
                device_id_type=MESH,
            ).wait_recv()
        total = gath[0, first : first + count].astype(F32)
        for time in range(1, nt):
            total += gath[time, first : first + count].astype(F32)
        fin[first : first + count] = total

    def deliver(kind):
        if kind == 0:
            src, dst = fin.at[pl.ds(0, 3)], res.at[pl.ds(0, 3), pl.ds(half * c, half), :]
            device = at(q - 1, 1, t)
        elif kind == 1:
            src, dst = fin.at[pl.ds(3, 2)], res.at[pl.ds(0, 2), pl.ds(half * c, half), :]
            device = at(q, 0, t)
        else:
            src, dst = fin.at[pl.ds(5, 1)], res.at[pl.ds(2, 1), pl.ds(half * c, half), :]
            device = at(q, 0, t)
        return pltpu.make_async_remote_copy(
            src_ref=src,
            dst_ref=dst,
            send_sem=fsend.at[kind],
            recv_sem=frecv.at[kind, c],
            device_id=device,
            device_id_type=MESH,
        )

    def delivered(kind, core):
        first, count = ((0, 3), (3, 2), (5, 1))[kind]
        pltpu.make_async_remote_copy(
            src_ref=fin.at[pl.ds(first, count)],
            dst_ref=res.at[pl.ds(2 if kind == 2 else 0, count), pl.ds(half * core, half), :],
            send_sem=fsend.at[kind],
            recv_sem=frecv.at[kind, core],
            device_id=at(q, 1 - c, t),
            device_id_type=MESH,
        ).wait_recv()

    acc[...] = jnp.zeros(acc.shape, F32)

    whiten([(mine, 0, 8)])
    arrive(theirs, 0)
    halo_wait(mine)
    whiten([(mine, 8, 8)])
    arrive(theirs, 1)
    whiten([(theirs, 0, 8)])
    cross([(3, SLOT_B, SLOT_C)], 0, 8)
    arrive(theirs, 2)
    arrive(theirs, 3)

    def arrive_sides(k):
        @pl.when(below)
        def _():
            arrive(SLOT_A, k)

        @pl.when(above)
        def _():
            arrive(SLOT_D, k)

    halo_wait(theirs)
    whiten([(theirs, 8, 8)])
    cross([(3, SLOT_B, SLOT_C)], 8, 8)

    for k in range(steps):
        arrive_sides(k)

        @pl.when(c == 0)
        def _():
            main_left(k)
            if k + 2 < steps:
                main_start(k + 2)

        if k + 2 >= steps:
            edge_start(2 * (k + 2 - steps))
            edge_start(2 * (k + 2 - steps) + 1)
        if k == steps - 1:
            @pl.when(below)
            def _():
                halo_wait(SLOT_A)

            @pl.when(above)
            def _():
                halo_wait(SLOT_D)

        whiten([(SLOT_A, 4 * k, 4), (SLOT_D, 4 * k, 4)])
        cross(
            [(0, SLOT_A, SLOT_B), (1, SLOT_A, SLOT_C), (2, SLOT_A, SLOT_D), (4, SLOT_B, SLOT_D)],
            4 * k,
            4,
        )

    lags_of(0, 5)
    for d in range(1, nt):
        exchange(0, 0, 5, d).start()


    for k in range(steps):
        @pl.when(above)
        def _():
            arrive(SLOT_E, k)
            if k == steps - 1:
                halo_wait(SLOT_E)

        whiten([(SLOT_E, 4 * k, 4)])
        cross([(5, SLOT_B, SLOT_E)], 4 * k, 4)

    lags_of(5, 1)
    for d in range(1, nt):
        exchange(1, 5, 1, d).start()

    collect(0, 0, 5)

    @pl.when(below)
    def _():
        deliver(0).start()

    @pl.when(c == 1)
    def _():
        deliver(1).start()

    @pl.when(c == 0)
    def _():
        res[0:2, 0:half] = fin[3:5]

    collect(1, 5, 1)

    @pl.when(c == 1)
    def _():
        deliver(2).start()

    @pl.when(c == 0)
    def _():
        res[2, 0:half] = fin[5]
        delivered(1, 1)
        delivered(2, 1)

    @pl.when(jnp.logical_and(c == 1, above))
    def _():
        delivered(0, 0)
        delivered(0, 1)

    for slot in range(LIMIT):
        reach = partners[0, slot] - chan
        row = jnp.zeros((chans, cols), F32)
        for offset in range(LIMIT):
            row = jnp.where(reach == offset + 1, res[offset], row)
        out_ref[slot] = row

    for k in range(steps):
        stream(0, k).wait_send()

        @pl.when(c == 1)
        def _():
            main_left(k)

        @pl.when(edge_ok)
        def _():
            stream(3, k).wait_send()
            stream(4, k).wait_send()

    halos(lambda copy: copy.wait_send())

    for d in range(1, nt):
        exchange(0, 0, 5, d).wait_send()
        exchange(1, 5, 1, d).wait_send()

    @pl.when(below)
    def _():
        deliver(0).wait_send()

    @pl.when(c == 1)
    def _():
        deliver(1).wait_send()
        deliver(2).wait_send()


def solution(mesh):
    nq, nt = mesh.shape["chan"] // 2, mesh.shape["tm"]

    def per_device(traces, live_channels, partners):
        chans, samples = traces.shape
        half = chans // 2
        segs = samples // HOP
        steps = segs // 4
        cols = NFFT // nt
        anywhere = pl.BlockSpec(memory_space=pltpu.HBM)
        by_slot = pl.pallas_call(
            functools.partial(kernel, nq, nt, segs, chans),
            out_shape=jax.ShapeDtypeStruct((LIMIT, chans, cols), F32),
            in_specs=[anywhere] * 7,
            out_specs=pl.BlockSpec(memory_space=pltpu.VMEM),
            scratch_shapes=[
                pltpu.SMEM((1,), jnp.int32),
                pltpu.SMEM((1, LIMIT), jnp.int32),
                pltpu.VMEM((2, HOP), F32),
                pltpu.VMEM((segs, chans, HOP), BF16),
                pltpu.VMEM((5, segs + 1, half, HOP), BF16),
                pltpu.VMEM((5, segs, half, NFFT), BF16),
                pltpu.VMEM((PAIRS, half, NFFT), F32),
                pltpu.VMEM((2, HOP, HOP), BF16),
                pltpu.VMEM((HOP, HOP), BF16),
                pltpu.VMEM((2, HOP, HOP), BF16),
                pltpu.VMEM((nt, PAIRS, half, cols), BF16),
                pltpu.VMEM((nt, PAIRS, half, cols), BF16),
                pltpu.VMEM((PAIRS, half, cols), F32),
                pltpu.VMEM((LIMIT, chans, cols), F32),
                pltpu.SemaphoreType.DMA((segs,)),
                pltpu.SemaphoreType.DMA((6,)),
                pltpu.SemaphoreType.DMA((5, steps)),
                pltpu.SemaphoreType.DMA((5, steps)),
                pltpu.SemaphoreType.DMA((6,)),
                pltpu.SemaphoreType.DMA((5,)),
                pltpu.SemaphoreType.DMA((2, nt)),
                pltpu.SemaphoreType.DMA((2, nt)),
                pltpu.SemaphoreType.DMA((3,)),
                pltpu.SemaphoreType.DMA((3, 2)),
            ],
            compiler_params=pltpu.CompilerParams(
                collective_id=0, has_side_effects=True, vmem_limit_bytes=56 * 1024 * 1024
            ),
        )(
            live_channels,
            partners,
            traces,
            jnp.asarray(taper_rows()),
            jnp.asarray(forward_tables()),
            jnp.asarray(band_table()),
            jnp.asarray(lag_tables(segs * nt)),
        )
        return by_slot.transpose(1, 0, 2)

    in_specs = (P("chan", "tm"), P("chan"), P("chan", None))
    out_specs = P("chan", None, "tm")
    return jax.shard_map(
        per_device, mesh=mesh, in_specs=in_specs, out_specs=out_specs, check_vma=False
    )
```

```python
import functools
import math

import jax
import jax.numpy as jnp
import ml_dtypes
import numpy as np
from jax import lax
from jax.experimental import pallas as pl
from jax.experimental.pallas import tpu as pltpu
from jax.sharding import PartitionSpec as P

NFFT = 1024
HOP = NFFT // 2
SMOOTH = 64
LIMIT = 3
MESH = pl.DeviceIdType.MESH
F32 = jnp.float32
BF16 = jnp.bfloat16

SLOT_A, SLOT_B, SLOT_C, SLOT_D, SLOT_E, SLOT_G = range(6)
PAIRS = 9


def bin_order():
    return np.concatenate([np.arange(2, HOP + 1, 2), np.arange(1, HOP, 2)])


def taper_rows():
    steps = np.arange(NFFT, dtype=np.float64)
    return (0.5 - 0.5 * np.cos(steps * (2.0 * math.pi / NFFT))).astype(np.float32).reshape(2, HOP)


def forward_tables():
    samples = np.arange(HOP)[:, None]
    tables = []
    for bins in (bin_order()[None, : HOP // 2], bin_order()[None, HOP // 2 :]):
        phase = (samples * bins % NFFT) * (2.0 * math.pi / NFFT)
        tables.append(np.concatenate([np.cos(phase), -np.sin(phase)], 1))
    return np.stack(tables).astype(ml_dtypes.bfloat16)


def band_table():
    freqs = bin_order() - 1
    start = np.clip(freqs - SMOOTH // 2, 0, HOP - SMOOTH)[None, :]
    source = freqs[:, None]
    return (((source >= start) & (source < start + SMOOTH)) / SMOOTH).astype(ml_dtypes.bfloat16)


def lag_tables(segments):
    shifts = np.arange(HOP)[None, :]
    tables = []
    for bins in (bin_order()[: HOP // 2, None], bin_order()[HOP // 2 :, None]):
        phase = (bins * shifts % NFFT) * (2.0 * math.pi / NFFT)
        weight = np.where(bins < HOP, 2.0, 1.0) / math.sqrt(NFFT) / segments
        tables.append(np.concatenate([weight * np.cos(phase), -weight * np.sin(phase)], 0))
    return np.stack(tables).astype(ml_dtypes.bfloat16)


def chunk_bounds(segs):
    bounds = [(4 * s + 1, 4 * s + 5) for s in range(segs // 4)]
    bounds[0] = (0, 5)
    bounds[-1] = (bounds[-1][0], segs)
    return bounds


def kernel(
    nq, nt, segs, chans,
    live_hbm, partners_hbm, x_ref, taper_hbm, fwd_hbm, band_hbm, lag_hbm, out_ref,
    live, partners, taper, own, buf, white, acc, fwd, band, lagt, part, gath, fin, res,
    load_sem, table_sem, ssem, rsem, hsend, hrecv, asend, arecv, fsend, frecv,
):
    half = chans // 2
    steps = segs // 4
    cols = NFFT // nt
    chunks = chunk_bounds(segs)
    chan = lax.axis_index("chan")
    t = lax.axis_index("tm")
    q = chan // 2
    c = lax.rem(chan, 2)
    below, above = q > 0, q < nq - 1
    corner = q == nq - 2
    from_below = jnp.logical_and(q > 0, q < nq - 1)
    incoming = jnp.logical_and(q < nq - 1, c + q > 0)
    mine = SLOT_B + c
    theirs = SLOT_C - c

    def at(chip, core, time):
        return {"chan": 2 * chip + core, "tm": time}

    for h in range(segs):
        pltpu.make_async_copy(x_ref.at[:, pl.ds(HOP * h, HOP)], own.at[h], load_sem.at[h]).start()
    tables = [
        pltpu.make_async_copy(fwd_hbm, fwd, table_sem.at[0]),
        pltpu.make_async_copy(band_hbm, band, table_sem.at[1]),
        pltpu.make_async_copy(lag_hbm, lagt, table_sem.at[2]),
        pltpu.make_async_copy(taper_hbm, taper, table_sem.at[3]),
        pltpu.make_async_copy(partners_hbm, partners, table_sem.at[4]),
    ]
    live_copy = pltpu.make_async_copy(live_hbm, live, table_sem.at[5])
    live_copy.start()
    for copy in tables:
        copy.start()

    @pl.when(jnp.logical_not(from_below))
    def _():
        buf[SLOT_A] = jnp.zeros((segs + 1, half, HOP), BF16)

    @pl.when(q == nq - 1)
    def _():
        buf[SLOT_D] = jnp.zeros((segs + 1, half, HOP), BF16)

    @pl.when(q >= nq - 2)
    def _():
        res[...] = jnp.zeros(res.shape, F32)

    @pl.when(jnp.logical_not(incoming))
    def _():
        buf[SLOT_E] = jnp.zeros((segs + 1, half, HOP), BF16)

    @pl.when(t == nt - 1)
    def _():
        for slot in range(6):
            buf[slot, segs] = jnp.zeros((half, HOP), BF16)

    barrier = pltpu.get_barrier_semaphore()

    def greet(chip, core, time):
        pl.semaphore_signal(barrier, inc=1, device_id=at(chip, core, time), device_id_type=MESH)

    for d in range(1, nt):
        greet(q, c, lax.rem(t + d, nt))

    def greet_around(time):
        greet(q, 1 - c, time)

        @pl.when(below)
        def _():
            greet(q - 1, 0, time)
            greet(q - 1, 1, time)

        @pl.when(above)
        def _():
            greet(q + 1, 0, time)
            greet(q + 1, 1, time)

    greet_around(t)

    @pl.when(t > 0)
    def _():
        greet_around(t - 1)

    @pl.when(t < nt - 1)
    def _():
        greet_around(t + 1)

    live_copy.wait()
    alive = lax.broadcasted_iota(jnp.int32, (chans, HOP), 0) < live[0]
    mask = jnp.where(alive, F32(1.0), F32(0.0)).astype(BF16)

    def mask_one(h, carry):
        pltpu.make_async_copy(
            x_ref.at[:, pl.ds(pl.multiple_of(HOP * h, HOP), HOP)], own.at[h], load_sem.at[h]
        ).wait()
        own[h] = own[h] * mask
        buf[mine, h] = own[h, pl.ds(pl.multiple_of(half * c, half), half), :]
        return carry

    lax.fori_loop(0, segs, mask_one, 0)

    around = 1 + 2 * jnp.where(below, 1, 0) + 2 * jnp.where(above, 1, 0)
    times = 1 + jnp.where(t > 0, 1, 0) + jnp.where(t < nt - 1, 1, 0)
    pl.semaphore_wait(barrier, nt - 1 + around * times)

    outward = 2 * c - 1
    main_ok = jnp.where(c == 0, q, nq - 2 - q) > 0
    edge_ok = jnp.where(c == 0, nq - 2 - q, q) > 0
    extra_ok = jnp.logical_and(c == 1, q == nq - 1)

    def route(index):
        if index == 0:
            return half * (1 - c), mine, q, 1 - c
        if index in (1, 2):
            return half * (index - 1), 3 * (1 - c), q + outward, index - 1
        if index == 3:
            return half * c, SLOT_E, q - outward, c
        if index == 5:
            return 0, SLOT_G, q - 1, 0
        return half * c, mine, q, c

    def stream(index, k):
        lo, hi = chunks[k]
        row, slot, chip, core = route(index)
        return pltpu.make_async_remote_copy(
            src_ref=own.at[pl.ds(lo, hi - lo), pl.ds(row, half), :],
            dst_ref=buf.at[slot, pl.ds(lo, hi - lo)],
            send_sem=ssem.at[index, k],
            recv_sem=rsem.at[slot, k],
            device_id=at(chip, core, t),
            device_id_type=MESH,
        )

    def halo(index):
        row, slot, chip, core = route(index)
        return pltpu.make_async_remote_copy(
            src_ref=own.at[0, pl.ds(row, half), :],
            dst_ref=buf.at[slot, segs],
            send_sem=hsend.at[index],
            recv_sem=hrecv.at[slot],
            device_id=at(chip, core, t - 1),
            device_id_type=MESH,
        )

    def halos(act):
        @pl.when(t > 0)
        def _():
            act(halo(4))
            act(halo(0))

            @pl.when(main_ok)
            def _():
                act(halo(1))
                act(halo(2))

            @pl.when(edge_ok)
            def _():
                act(halo(3))

            @pl.when(extra_ok)
            def _():
                act(halo(5))

    def arrive(slot, k):
        lo, hi = chunks[k]
        pltpu.make_async_remote_copy(
            src_ref=own.at[pl.ds(lo, hi - lo), pl.ds(0, half), :],
            dst_ref=buf.at[slot, pl.ds(lo, hi - lo)],
            send_sem=ssem.at[0, k],
            recv_sem=rsem.at[slot, k],
            device_id=at(q, 1 - c, t),
            device_id_type=MESH,
        ).wait_recv()

    def halo_wait(slot):
        @pl.when(t < nt - 1)
        def _():
            pltpu.make_async_remote_copy(
                src_ref=own.at[0, pl.ds(0, half), :],
                dst_ref=buf.at[slot, segs],
                send_sem=hsend.at[0],
                recv_sem=hrecv.at[slot],
                device_id=at(q, c, t + 1),
                device_id_type=MESH,
            ).wait_recv()

    def main_start(k):
        @pl.when(main_ok)
        def _():
            stream(1, k).start()
            stream(2, k).start()

    def main_left(k):
        @pl.when(main_ok)
        def _():
            stream(1, k).wait_send()
            stream(2, k).wait_send()

    def edge_start(k):
        @pl.when(edge_ok)
        def _():
            stream(3, k).start()

        @pl.when(extra_ok)
        def _():
            stream(5, k).start()

    stream(0, 0).start()
    main_start(0)
    halos(lambda copy: copy.start())
    for k in range(1, steps):
        stream(0, k).start()
    main_start(1)

    for copy in tables:
        copy.wait()

    taper_rise, taper_fall = taper[0:1, :], taper[1:2, :]
    quarter = HOP // 2

    def whiten(parts):
        sums, differences = [], []
        for slot, first, count in parts:
            samples = buf[slot, first : first + count + 1].astype(F32)
            rise, fall = samples[:count] * taper_rise, samples[1:] * taper_fall
            sums.append((rise + fall).astype(BF16).reshape(count * half, HOP))
            differences.append((rise - fall).astype(BF16).reshape(count * half, HOP))
        even = jnp.dot(jnp.concatenate(sums, 0), fwd[0], preferred_element_type=F32)
        odd = jnp.dot(jnp.concatenate(differences, 0), fwd[1], preferred_element_type=F32)
        power = [
            (z[:, :quarter] * z[:, :quarter] + z[:, quarter:] * z[:, quarter:]).astype(BF16)
            for z in (even, odd)
        ]
        smooth = jnp.dot(jnp.concatenate(power, 1), band[...], preferred_element_type=F32)
        factor = lax.rsqrt(smooth + 1e-06)
        row = 0
        for slot, first, count in parts:
            rows = slice(row, row + count * half)
            row += count * half
            for n, z in enumerate((even, odd)):
                scale = factor[rows, n * quarter : (n + 1) * quarter]
                for m in range(2):
                    value = (z[rows, m * quarter : (m + 1) * quarter] * scale).astype(BF16)
                    lanes = slice(m * HOP + n * quarter, m * HOP + (n + 1) * quarter)
                    white[slot, first : first + count, :, lanes] = value.reshape(count, half, quarter)

    def cross(pairs, start, count):
        slots = []
        for _, first, second in pairs:
            for slot in (first, second):
                if not any(slot is s for s in slots):
                    slots.append(slot)

        def tile(i, carry):
            rows = pl.ds(pl.multiple_of(16 * (i // 4), 16), 16)
            lanes = pl.multiple_of(128 * lax.rem(i, 4), 128)
            lanes_re, lanes_im = pl.ds(lanes, 128), pl.ds(HOP + lanes, 128)
            sums = [[acc[p, rows, lanes_re], acc[p, rows, lanes_im]] for p, _, _ in pairs]
            for seg in range(start, start + count):
                values = [
                    (
                        white[slot, seg, rows, lanes_re].astype(F32),
                        white[slot, seg, rows, lanes_im].astype(F32),
                    )
                    for slot in slots
                ]
                for n, (_, first, second) in enumerate(pairs):
                    a_re, a_im = [v for s, v in zip(slots, values) if s is first][0]
                    b_re, b_im = [v for s, v in zip(slots, values) if s is second][0]
                    sums[n][0] += a_re * b_re + a_im * b_im
                    sums[n][1] += a_im * b_re - a_re * b_im
            for n, (p, _, _) in enumerate(pairs):
                acc[p, rows, lanes_re] = sums[n][0]
                acc[p, rows, lanes_im] = sums[n][1]
            return carry

        lax.fori_loop(0, (half // 16) * 4, tile, 0)

    def lags_of(first, count):
        stack = acc[first : first + count].reshape(count * half, NFFT)
        high = stack.astype(BF16)
        low = (stack - high.astype(F32)).astype(BF16)
        both = jnp.concatenate([high, low], 0)
        sides = []
        for n in range(2):
            lanes = slice(n * quarter, (n + 1) * quarter)
            lanes_im = slice(HOP + n * quarter, HOP + (n + 1) * quarter)
            side = jnp.dot(
                jnp.concatenate([both[:, lanes], both[:, lanes_im]], 1),
                lagt[n],
                preferred_element_type=F32,
            )
            sides.append(side[: count * half] + side[count * half :])
        even, odd = sides
        lags = jnp.concatenate([(even + odd).astype(BF16), (even - odd).astype(BF16)], 1)
        for time in range(nt):
            part[time, first : first + count] = lags[:, time * cols : (time + 1) * cols].reshape(
                count, half, cols
            )

    def exchange(group, first, count, d):
        peer = lax.rem(t + d, nt)
        return pltpu.make_async_remote_copy(
            src_ref=part.at[peer, pl.ds(first, count)],
            dst_ref=gath.at[t, pl.ds(first, count)],
            send_sem=asend.at[group, d],
            recv_sem=arecv.at[group, t],
            device_id=at(q, c, peer),
            device_id_type=MESH,
        )

    def collect(group, first, count):
        gath[t, first : first + count] = part[t, first : first + count]
        for d in range(1, nt):
            source = lax.rem(t + d, nt)
            pltpu.make_async_remote_copy(
                src_ref=part.at[source, pl.ds(first, count)],
                dst_ref=gath.at[source, pl.ds(first, count)],
                send_sem=asend.at[group, d],
                recv_sem=arecv.at[group, source],
                device_id=at(q, c, source),
                device_id_type=MESH,
            ).wait_recv()
        total = gath[0, first : first + count].astype(F32)
        for time in range(1, nt):
            total += gath[time, first : first + count].astype(F32)
        fin[first : first + count] = total

    def deliver(kind):
        if kind == 0:
            src, dst = fin.at[pl.ds(0, 3)], res.at[pl.ds(0, 3), pl.ds(half * c, half), :]
            device = at(q - 1, 1, t)
        elif kind == 3:
            src, dst = fin.at[pl.ds(6, 2)], res.at[pl.ds(0, 2), pl.ds(0, half), :]
            device = at(q, 1, t)
        elif kind == 1:
            src, dst = fin.at[pl.ds(3, 2)], res.at[pl.ds(0, 2), pl.ds(half * c, half), :]
            device = at(q, 0, t)
        else:
            src, dst = fin.at[pl.ds(5, 1)], res.at[pl.ds(2, 1), pl.ds(half * c, half), :]
            device = at(jnp.where(c == 0, q - 1, q), 0, t)
        return pltpu.make_async_remote_copy(
            src_ref=src,
            dst_ref=dst,
            send_sem=fsend.at[kind],
            recv_sem=frecv.at[kind, c],
            device_id=device,
            device_id_type=MESH,
        )

    def delivered(kind, core):
        first, count = ((0, 3), (3, 2), (5, 1), (6, 2))[kind]
        pltpu.make_async_remote_copy(
            src_ref=fin.at[pl.ds(first, count)],
            dst_ref=res.at[pl.ds(2 if kind == 2 else 0, count), pl.ds(half * core, half), :],
            send_sem=fsend.at[kind],
            recv_sem=frecv.at[kind, core],
            device_id=at(q, 1 - c, t),
            device_id_type=MESH,
        ).wait_recv()

    acc[...] = jnp.zeros(acc.shape, F32)

    whiten([(mine, 0, 8)])
    arrive(theirs, 0)
    halo_wait(mine)
    whiten([(mine, 8, 8)])
    arrive(theirs, 1)
    whiten([(theirs, 0, 8)])
    cross([(3, SLOT_B, SLOT_C)], 0, 8)
    arrive(theirs, 2)
    arrive(theirs, 3)

    def arrive_sides(k):
        @pl.when(from_below)
        def _():
            arrive(SLOT_A, k)

        @pl.when(above)
        def _():
            arrive(SLOT_D, k)

    halo_wait(theirs)
    whiten([(theirs, 8, 8)])
    cross([(3, SLOT_B, SLOT_C)], 8, 8)

    for k in range(steps):
        main_left(k)
        if k + 2 < steps:
            main_start(k + 2)
        else:
            edge_start(2 * (k + 2 - steps))
            edge_start(2 * (k + 2 - steps) + 1)
        arrive_sides(k)
        if k == steps - 1:
            @pl.when(from_below)
            def _():
                halo_wait(SLOT_A)

            @pl.when(above)
            def _():
                halo_wait(SLOT_D)

        whiten([(SLOT_A, 4 * k, 4), (SLOT_D, 4 * k, 4)])
        cross(
            [(0, SLOT_A, SLOT_B), (1, SLOT_A, SLOT_C), (2, SLOT_A, SLOT_D), (4, SLOT_B, SLOT_D)],
            4 * k,
            4,
        )

    lags_of(0, 5)
    for d in range(1, nt):
        exchange(0, 0, 5, d).start()

    first_white = jnp.where(c == 0, SLOT_E, SLOT_B)
    second_white = jnp.where(c == 0, SLOT_C, SLOT_E)

    for k in range(steps):
        @pl.when(incoming)
        def _():
            arrive(SLOT_E, k)
            if k == steps - 1:
                halo_wait(SLOT_E)

        whiten([(SLOT_E, 4 * k, 4)])
        cross([(5, first_white, second_white)], 4 * k, 4)

    lags_of(5, 1)
    for d in range(1, nt):
        exchange(1, 5, 1, d).start()

    second = jnp.where(c == 0, SLOT_G, SLOT_E)

    @pl.when(corner)
    def _():
        @pl.when(c == 0)
        def _():
            for k in range(steps):
                arrive(SLOT_G, k)
            halo_wait(SLOT_G)
            whiten([(SLOT_G, 0, 8)])
            whiten([(SLOT_G, 8, 8)])

        pairs = [(6, SLOT_C, SLOT_D), (7, SLOT_C, second), (8, SLOT_B, second)]
        cross(pairs, 0, 8)
        cross(pairs, 8, 8)
        lags_of(6, 3)
        for d in range(1, nt):
            exchange(2, 6, 3, d).start()

    collect(0, 0, 5)

    @pl.when(from_below)
    def _():
        deliver(0).start()

    @pl.when(c == 1)
    def _():
        deliver(1).start()

    @pl.when(c == 0)
    def _():
        res[0:2, 0:half] = fin[3:5]

    collect(1, 5, 1)
    last_ok = jnp.logical_or(c == 1, from_below)

    @pl.when(last_ok)
    def _():
        deliver(2).start()

    @pl.when(corner)
    def _():
        collect(2, 6, 3)

        @pl.when(c == 0)
        def _():
            deliver(3).start()
            res[2, 0:half] = fin[8]

        @pl.when(c == 1)
        def _():
            res[0:2, half:chans] = fin[6:8]
            delivered(3, 0)

    @pl.when(c == 0)
    def _():
        delivered(1, 1)
        delivered(2, 1)

    @pl.when(q < nq - 2)
    def _():
        @pl.when(c == 0)
        def _():
            delivered(2, 0)

        @pl.when(c == 1)
        def _():
            delivered(0, 0)
            delivered(0, 1)

    for slot in range(LIMIT):
        reach = partners[0, slot] - chan
        row = jnp.zeros((chans, cols), F32)
        for offset in range(LIMIT):
            row = jnp.where(reach == offset + 1, res[offset], row)
        out_ref[slot] = row

    for k in range(steps):
        stream(0, k).wait_send()

        @pl.when(edge_ok)
        def _():
            stream(3, k).wait_send()

        @pl.when(extra_ok)
        def _():
            stream(5, k).wait_send()

    halos(lambda copy: copy.wait_send())

    for d in range(1, nt):
        exchange(0, 0, 5, d).wait_send()
        exchange(1, 5, 1, d).wait_send()

    @pl.when(corner)
    def _():
        for d in range(1, nt):
            exchange(2, 6, 3, d).wait_send()

        @pl.when(c == 0)
        def _():
            deliver(3).wait_send()

    @pl.when(from_below)
    def _():
        deliver(0).wait_send()

    @pl.when(c == 1)
    def _():
        deliver(1).wait_send()

    @pl.when(last_ok)
    def _():
        deliver(2).wait_send()


def solution(mesh):
    nq, nt = mesh.shape["chan"] // 2, mesh.shape["tm"]

    def per_device(traces, live_channels, partners):
        chans, samples = traces.shape
        half = chans // 2
        segs = samples // HOP
        steps = segs // 4
        cols = NFFT // nt
        anywhere = pl.BlockSpec(memory_space=pltpu.HBM)
        by_slot = pl.pallas_call(
            functools.partial(kernel, nq, nt, segs, chans),
            out_shape=jax.ShapeDtypeStruct((LIMIT, chans, cols), F32),
            in_specs=[anywhere] * 7,
            out_specs=pl.BlockSpec(memory_space=pltpu.VMEM),
            scratch_shapes=[
                pltpu.SMEM((1,), jnp.int32),
                pltpu.SMEM((1, LIMIT), jnp.int32),
                pltpu.VMEM((2, HOP), F32),
                pltpu.VMEM((segs, chans, HOP), BF16),
                pltpu.VMEM((6, segs + 1, half, HOP), BF16),
                pltpu.VMEM((6, segs, half, NFFT), BF16),
                pltpu.VMEM((PAIRS, half, NFFT), F32),
                pltpu.VMEM((2, HOP, HOP), BF16),
                pltpu.VMEM((HOP, HOP), BF16),
                pltpu.VMEM((2, HOP, HOP), BF16),
                pltpu.VMEM((nt, PAIRS, half, cols), BF16),
                pltpu.VMEM((nt, PAIRS, half, cols), BF16),
                pltpu.VMEM((PAIRS, half, cols), F32),
                pltpu.VMEM((LIMIT, chans, cols), F32),
                pltpu.SemaphoreType.DMA((segs,)),
                pltpu.SemaphoreType.DMA((6,)),
                pltpu.SemaphoreType.DMA((6, steps)),
                pltpu.SemaphoreType.DMA((6, steps)),
                pltpu.SemaphoreType.DMA((6,)),
                pltpu.SemaphoreType.DMA((6,)),
                pltpu.SemaphoreType.DMA((3, nt)),
                pltpu.SemaphoreType.DMA((3, nt)),
                pltpu.SemaphoreType.DMA((4,)),
                pltpu.SemaphoreType.DMA((4, 2)),
            ],
            compiler_params=pltpu.CompilerParams(
                collective_id=0, has_side_effects=True, vmem_limit_bytes=56 * 1024 * 1024
            ),
        )(
            live_channels,
            partners,
            traces,
            jnp.asarray(taper_rows()),
            jnp.asarray(forward_tables()),
            jnp.asarray(band_table()),
            jnp.asarray(lag_tables(segs * nt)),
        )
        return by_slot.transpose(1, 0, 2)

    in_specs = (P("chan", "tm"), P("chan"), P("chan", None))
    out_specs = P("chan", None, "tm")
    return jax.shard_map(
        per_device, mesh=mesh, in_specs=in_specs, out_specs=out_specs, check_vma=False
    )
```

```python
import functools
import math

import jax
import jax.numpy as jnp
import ml_dtypes
import numpy as np
from jax import lax
from jax.experimental import pallas as pl
from jax.experimental.pallas import tpu as pltpu
from jax.sharding import PartitionSpec as P

NFFT = 1024
HOP = NFFT // 2
SMOOTH = 64
LIMIT = 3
MESH = pl.DeviceIdType.MESH
F32 = jnp.float32
BF16 = jnp.bfloat16

SLOT_A, SLOT_B, SLOT_C, SLOT_D, SLOT_E = range(5)
PAIRS = 8


def bin_order():
    return np.concatenate([np.arange(2, HOP + 1, 2), np.arange(1, HOP, 2)])


def taper_rows():
    steps = np.arange(NFFT, dtype=np.float64)
    return (0.5 - 0.5 * np.cos(steps * (2.0 * math.pi / NFFT))).astype(np.float32).reshape(2, HOP)


def forward_tables():
    samples = np.arange(HOP)[:, None]
    tables = []
    for bins in (bin_order()[None, : HOP // 2], bin_order()[None, HOP // 2 :]):
        phase = (samples * bins % NFFT) * (2.0 * math.pi / NFFT)
        tables.append(np.concatenate([np.cos(phase), -np.sin(phase)], 1))
    return np.stack(tables).astype(ml_dtypes.bfloat16)


def band_table():
    freqs = bin_order() - 1
    start = np.clip(freqs - SMOOTH // 2, 0, HOP - SMOOTH)[None, :]
    source = freqs[:, None]
    return (((source >= start) & (source < start + SMOOTH)) / SMOOTH).astype(ml_dtypes.bfloat16)


def lag_tables(segments):
    shifts = np.arange(HOP)[None, :]
    tables = []
    for bins in (bin_order()[: HOP // 2, None], bin_order()[HOP // 2 :, None]):
        phase = (bins * shifts % NFFT) * (2.0 * math.pi / NFFT)
        weight = np.where(bins < HOP, 2.0, 1.0) / math.sqrt(NFFT) / segments
        tables.append(np.concatenate([weight * np.cos(phase), -weight * np.sin(phase)], 0))
    return np.stack(tables).astype(ml_dtypes.bfloat16)


def chunk_bounds(segs):
    bounds = [(4 * s + 1, 4 * s + 5) for s in range(segs // 4)]
    bounds[0] = (0, 5)
    bounds[-1] = (bounds[-1][0], segs)
    return bounds


def kernel(
    nq, nt, segs, chans,
    live_hbm, partners_hbm, x_ref, taper_hbm, fwd_hbm, band_hbm, lag_hbm, out_ref,
    live, partners, taper, own, buf, white, acc, fwd, band, lagt, part, gath, fin, res,
    load_sem, table_sem, ssem, rsem, hsend, hrecv, asend, arecv, fsend, frecv,
):
    half = chans // 2
    steps = segs // 4
    cols = NFFT // nt
    chunks = chunk_bounds(segs)
    chan = lax.axis_index("chan")
    t = lax.axis_index("tm")
    q = chan // 2
    c = lax.rem(chan, 2)
    below, above = q > 0, q < nq - 1
    corner = jnp.logical_and(q == nq - 2, c == 1)
    from_below = jnp.logical_and(q > 0, q + c < nq)
    incoming = jnp.where(c == 0, q, nq - 1 - q) > 0
    mine = SLOT_B + c
    theirs = SLOT_C - c

    def at(chip, core, time):
        return {"chan": 2 * chip + core, "tm": time}

    for h in range(segs):
        pltpu.make_async_copy(x_ref.at[:, pl.ds(HOP * h, HOP)], own.at[h], load_sem.at[h]).start()
    tables = [
        pltpu.make_async_copy(fwd_hbm, fwd, table_sem.at[0]),
        pltpu.make_async_copy(band_hbm, band, table_sem.at[1]),
        pltpu.make_async_copy(lag_hbm, lagt, table_sem.at[2]),
        pltpu.make_async_copy(taper_hbm, taper, table_sem.at[3]),
        pltpu.make_async_copy(partners_hbm, partners, table_sem.at[4]),
    ]
    live_copy = pltpu.make_async_copy(live_hbm, live, table_sem.at[5])
    live_copy.start()
    for copy in tables:
        copy.start()

    @pl.when(jnp.logical_not(from_below))
    def _():
        buf[SLOT_A] = jnp.zeros((segs + 1, half, HOP), BF16)

    @pl.when(q == nq - 1)
    def _():
        buf[SLOT_D] = jnp.zeros((segs + 1, half, HOP), BF16)

    @pl.when(q >= nq - 2)
    def _():
        res[...] = jnp.zeros(res.shape, F32)

    @pl.when(jnp.logical_not(incoming))
    def _():
        buf[SLOT_E] = jnp.zeros((segs + 1, half, HOP), BF16)

    @pl.when(t == nt - 1)
    def _():
        for slot in range(5):
            buf[slot, segs] = jnp.zeros((half, HOP), BF16)

    barrier = pltpu.get_barrier_semaphore()

    def greet(chip, core, time):
        pl.semaphore_signal(barrier, inc=1, device_id=at(chip, core, time), device_id_type=MESH)

    for d in range(1, nt):
        greet(q, c, lax.rem(t + d, nt))

    def greet_around(time):
        greet(q, 1 - c, time)

        @pl.when(below)
        def _():
            greet(q - 1, 0, time)
            greet(q - 1, 1, time)

        @pl.when(above)
        def _():
            greet(q + 1, 0, time)
            greet(q + 1, 1, time)

    greet_around(t)

    @pl.when(t > 0)
    def _():
        greet_around(t - 1)

    @pl.when(t < nt - 1)
    def _():
        greet_around(t + 1)

    live_copy.wait()
    alive = lax.broadcasted_iota(jnp.int32, (chans, HOP), 0) < live[0]
    mask = jnp.where(alive, F32(1.0), F32(0.0)).astype(BF16)

    def mask_one(h, carry):
        pltpu.make_async_copy(
            x_ref.at[:, pl.ds(pl.multiple_of(HOP * h, HOP), HOP)], own.at[h], load_sem.at[h]
        ).wait()
        own[h] = own[h] * mask
        buf[mine, h] = own[h, pl.ds(pl.multiple_of(half * c, half), half), :]
        return carry

    lax.fori_loop(0, segs, mask_one, 0)

    around = 1 + 2 * jnp.where(below, 1, 0) + 2 * jnp.where(above, 1, 0)
    times = 1 + jnp.where(t > 0, 1, 0) + jnp.where(t < nt - 1, 1, 0)
    pl.semaphore_wait(barrier, nt - 1 + around * times)

    outward = 2 * c - 1
    main_ok = (jnp.where(c == 0, q, nq - 1 - q) > 0, jnp.where(c == 0, q, nq - 2 - q) > 0)
    edge_ok = jnp.where(c == 0, nq - 1 - q, q) > 0

    def route(index):
        if index == 0:
            return half * (1 - c), mine, q, 1 - c
        if index in (1, 2):
            return half * (index - 1), 3 * (1 - c), q + outward, index - 1
        if index == 3:
            return half * c, SLOT_E, q - outward, c
        return half * c, mine, q, c

    def stream(index, k):
        lo, hi = chunks[k]
        row, slot, chip, core = route(index)
        return pltpu.make_async_remote_copy(
            src_ref=own.at[pl.ds(lo, hi - lo), pl.ds(row, half), :],
            dst_ref=buf.at[slot, pl.ds(lo, hi - lo)],
            send_sem=ssem.at[index, k],
            recv_sem=rsem.at[slot, k],
            device_id=at(chip, core, t),
            device_id_type=MESH,
        )

    def halo(index):
        row, slot, chip, core = route(index)
        return pltpu.make_async_remote_copy(
            src_ref=own.at[0, pl.ds(row, half), :],
            dst_ref=buf.at[slot, segs],
            send_sem=hsend.at[index],
            recv_sem=hrecv.at[slot],
            device_id=at(chip, core, t - 1),
            device_id_type=MESH,
        )

    def halos(act):
        @pl.when(t > 0)
        def _():
            act(halo(4))
            act(halo(0))

            for n in range(2):
                @pl.when(main_ok[n])
                def _():
                    act(halo(1 + n))

            @pl.when(edge_ok)
            def _():
                act(halo(3))

    def arrive(slot, k):
        lo, hi = chunks[k]
        pltpu.make_async_remote_copy(
            src_ref=own.at[pl.ds(lo, hi - lo), pl.ds(0, half), :],
            dst_ref=buf.at[slot, pl.ds(lo, hi - lo)],
            send_sem=ssem.at[0, k],
            recv_sem=rsem.at[slot, k],
            device_id=at(q, 1 - c, t),
            device_id_type=MESH,
        ).wait_recv()

    def halo_wait(slot):
        @pl.when(t < nt - 1)
        def _():
            pltpu.make_async_remote_copy(
                src_ref=own.at[0, pl.ds(0, half), :],
                dst_ref=buf.at[slot, segs],
                send_sem=hsend.at[0],
                recv_sem=hrecv.at[slot],
                device_id=at(q, c, t + 1),
                device_id_type=MESH,
            ).wait_recv()

    def main_start(k):
        for n in range(2):
            @pl.when(main_ok[n])
            def _():
                stream(1 + n, k).start()

    def main_left(k):
        for n in range(2):
            @pl.when(main_ok[n])
            def _():
                stream(1 + n, k).wait_send()

    def edge_start(k):
        @pl.when(edge_ok)
        def _():
            stream(3, k).start()

    stream(0, 0).start()
    main_start(0)
    halos(lambda copy: copy.start())
    for k in range(1, steps):
        stream(0, k).start()
    main_start(1)

    for copy in tables:
        copy.wait()

    taper_rise, taper_fall = taper[0:1, :], taper[1:2, :]
    quarter = HOP // 2

    def whiten(parts):
        sums, differences = [], []
        for slot, first, count in parts:
            samples = buf[slot, first : first + count + 1].astype(F32)
            rise, fall = samples[:count] * taper_rise, samples[1:] * taper_fall
            sums.append((rise + fall).astype(BF16).reshape(count * half, HOP))
            differences.append((rise - fall).astype(BF16).reshape(count * half, HOP))
        even = jnp.dot(jnp.concatenate(sums, 0), fwd[0], preferred_element_type=F32)
        odd = jnp.dot(jnp.concatenate(differences, 0), fwd[1], preferred_element_type=F32)
        power = [
            (z[:, :quarter] * z[:, :quarter] + z[:, quarter:] * z[:, quarter:]).astype(BF16)
            for z in (even, odd)
        ]
        smooth = jnp.dot(jnp.concatenate(power, 1), band[...], preferred_element_type=F32)
        factor = lax.rsqrt(smooth + 1e-06)
        row = 0
        for slot, first, count in parts:
            rows = slice(row, row + count * half)
            row += count * half
            for n, z in enumerate((even, odd)):
                scale = factor[rows, n * quarter : (n + 1) * quarter]
                for m in range(2):
                    value = (z[rows, m * quarter : (m + 1) * quarter] * scale).astype(BF16)
                    lanes = slice(m * HOP + n * quarter, m * HOP + (n + 1) * quarter)
                    white[slot, first : first + count, :, lanes] = value.reshape(count, half, quarter)

    def cross(pairs, start, count):
        slots = []
        for _, first, second in pairs:
            for slot in (first, second):
                if not any(slot is s for s in slots):
                    slots.append(slot)

        def tile(i, carry):
            rows = pl.ds(pl.multiple_of(16 * (i // 4), 16), 16)
            lanes = pl.multiple_of(128 * lax.rem(i, 4), 128)
            lanes_re, lanes_im = pl.ds(lanes, 128), pl.ds(HOP + lanes, 128)
            sums = [[acc[p, rows, lanes_re], acc[p, rows, lanes_im]] for p, _, _ in pairs]
            for seg in range(start, start + count):
                values = [
                    (
                        white[slot, seg, rows, lanes_re].astype(F32),
                        white[slot, seg, rows, lanes_im].astype(F32),
                    )
                    for slot in slots
                ]
                for n, (_, first, second) in enumerate(pairs):
                    a_re, a_im = [v for s, v in zip(slots, values) if s is first][0]
                    b_re, b_im = [v for s, v in zip(slots, values) if s is second][0]
                    sums[n][0] += a_re * b_re + a_im * b_im
                    sums[n][1] += a_im * b_re - a_re * b_im
            for n, (p, _, _) in enumerate(pairs):
                acc[p, rows, lanes_re] = sums[n][0]
                acc[p, rows, lanes_im] = sums[n][1]
            return carry

        lax.fori_loop(0, (half // 16) * 4, tile, 0)

    def lags_of(first, count):
        stack = acc[first : first + count].reshape(count * half, NFFT)
        high = stack.astype(BF16)
        low = (stack - high.astype(F32)).astype(BF16)
        both = jnp.concatenate([high, low], 0)
        sides = []
        for n in range(2):
            lanes = slice(n * quarter, (n + 1) * quarter)
            lanes_im = slice(HOP + n * quarter, HOP + (n + 1) * quarter)
            side = jnp.dot(
                jnp.concatenate([both[:, lanes], both[:, lanes_im]], 1),
                lagt[n],
                preferred_element_type=F32,
            )
            sides.append(side[: count * half] + side[count * half :])
        even, odd = sides
        lags = jnp.concatenate([(even + odd).astype(BF16), (even - odd).astype(BF16)], 1)
        for time in range(nt):
            part[time, first : first + count] = lags[:, time * cols : (time + 1) * cols].reshape(
                count, half, cols
            )

    def exchange(group, first, count, d):
        peer = lax.rem(t + d, nt)
        return pltpu.make_async_remote_copy(
            src_ref=part.at[peer, pl.ds(first, count)],
            dst_ref=gath.at[t, pl.ds(first, count)],
            send_sem=asend.at[group, d],
            recv_sem=arecv.at[group, t],
            device_id=at(q, c, peer),
            device_id_type=MESH,
        )

    def collect(group, first, count):
        gath[t, first : first + count] = part[t, first : first + count]
        for d in range(1, nt):
            source = lax.rem(t + d, nt)
            pltpu.make_async_remote_copy(
                src_ref=part.at[source, pl.ds(first, count)],
                dst_ref=gath.at[source, pl.ds(first, count)],
                send_sem=asend.at[group, d],
                recv_sem=arecv.at[group, source],
                device_id=at(q, c, source),
                device_id_type=MESH,
            ).wait_recv()
        total = gath[0, first : first + count].astype(F32)
        for time in range(1, nt):
            total += gath[time, first : first + count].astype(F32)
        fin[first : first + count] = total

    def deliver(kind):
        if kind == 0:
            src, dst = fin.at[pl.ds(0, 3)], res.at[pl.ds(0, 3), pl.ds(half * c, half), :]
            device = at(q - 1, 1, t)
        elif kind == 1:
            src, dst = fin.at[pl.ds(3, 2)], res.at[pl.ds(0, 2), pl.ds(half * c, half), :]
            device = at(q, 0, t)
        else:
            src, dst = fin.at[pl.ds(5, 1)], res.at[pl.ds(2, 1), pl.ds(half * c, half), :]
            device = at(jnp.where(c == 0, q - 1, q), 0, t)
        return pltpu.make_async_remote_copy(
            src_ref=src,
            dst_ref=dst,
            send_sem=fsend.at[kind],
            recv_sem=frecv.at[kind, c],
            device_id=device,
            device_id_type=MESH,
        )

    def delivered(kind, core):
        first, count = ((0, 3), (3, 2), (5, 1))[kind]
        pltpu.make_async_remote_copy(
            src_ref=fin.at[pl.ds(first, count)],
            dst_ref=res.at[pl.ds(2 if kind == 2 else 0, count), pl.ds(half * core, half), :],
            send_sem=fsend.at[kind],
            recv_sem=frecv.at[kind, core],
            device_id=at(q, 1 - c, t),
            device_id_type=MESH,
        ).wait_recv()

    acc[...] = jnp.zeros(acc.shape, F32)

    whiten([(mine, 0, 8)])
    arrive(theirs, 0)
    halo_wait(mine)
    whiten([(mine, 8, 8)])
    main_start(2)
    arrive(theirs, 1)
    whiten([(theirs, 0, 8)])
    cross([(3, SLOT_B, SLOT_C)], 0, 8)
    arrive(theirs, 2)
    arrive(theirs, 3)

    def arrive_sides(k):
        @pl.when(from_below)
        def _():
            arrive(SLOT_A, k)

        @pl.when(above)
        def _():
            arrive(SLOT_D, k)

    halo_wait(theirs)
    whiten([(theirs, 8, 8)])
    cross([(3, SLOT_B, SLOT_C)], 8, 8)

    for k in range(steps):
        main_left(k)
        if k + 3 < steps:
            main_start(k + 3)
        else:
            edge_start(k + 3 - steps)
        if k == steps - 1:
            edge_start(steps - 1)
        arrive_sides(k)
        if k == steps - 1:
            @pl.when(from_below)
            def _():
                halo_wait(SLOT_A)

            @pl.when(above)
            def _():
                halo_wait(SLOT_D)

        whiten([(SLOT_A, 4 * k, 4), (SLOT_D, 4 * k, 4)])
        cross(
            [(0, SLOT_A, SLOT_B), (1, SLOT_A, SLOT_C), (2, SLOT_A, SLOT_D), (4, SLOT_B, SLOT_D)],
            4 * k,
            4,
        )

    lags_of(0, 5)
    for d in range(1, nt):
        exchange(0, 0, 5, d).start()

    first_white = jnp.where(c == 0, SLOT_E, SLOT_B)
    second_white = jnp.where(c == 0, SLOT_C, SLOT_E)

    for k in range(steps):
        @pl.when(incoming)
        def _():
            arrive(SLOT_E, k)
            if k == steps - 1:
                halo_wait(SLOT_E)

        whiten([(SLOT_E, 4 * k, 4)])
        cross([(5, first_white, second_white)], 4 * k, 4)

    lags_of(5, 1)
    for d in range(1, nt):
        exchange(1, 5, 1, d).start()

    @pl.when(corner)
    def _():
        pairs = [(6, SLOT_C, SLOT_D), (7, SLOT_C, SLOT_E)]
        cross(pairs, 0, 8)
        cross(pairs, 8, 8)
        lags_of(6, 2)
        for d in range(1, nt):
            exchange(2, 6, 2, d).start()

    collect(0, 0, 5)

    @pl.when(from_below)
    def _():
        deliver(0).start()

    @pl.when(c == 1)
    def _():
        deliver(1).start()

    @pl.when(c == 0)
    def _():
        res[0:2, 0:half] = fin[3:5]

    collect(1, 5, 1)
    last_ok = jnp.logical_or(c == 1, from_below)

    @pl.when(last_ok)
    def _():
        deliver(2).start()

    @pl.when(corner)
    def _():
        collect(2, 6, 2)
        res[0:2, half:chans] = fin[6:8]

    @pl.when(c == 0)
    def _():
        delivered(1, 1)
        delivered(2, 1)

        @pl.when(above)
        def _():
            delivered(2, 0)

    @pl.when(jnp.logical_and(c == 1, above))
    def _():
        delivered(0, 0)

    @pl.when(jnp.logical_and(c == 1, q < nq - 2))
    def _():
        delivered(0, 1)

    for slot in range(LIMIT):
        reach = partners[0, slot] - chan
        row = jnp.zeros((chans, cols), F32)
        for offset in range(LIMIT):
            row = jnp.where(reach == offset + 1, res[offset], row)
        out_ref[slot] = row

    for k in range(steps):
        stream(0, k).wait_send()

        @pl.when(edge_ok)
        def _():
            stream(3, k).wait_send()

    halos(lambda copy: copy.wait_send())

    for d in range(1, nt):
        exchange(0, 0, 5, d).wait_send()
        exchange(1, 5, 1, d).wait_send()

    @pl.when(corner)
    def _():
        for d in range(1, nt):
            exchange(2, 6, 2, d).wait_send()

    @pl.when(from_below)
    def _():
        deliver(0).wait_send()

    @pl.when(c == 1)
    def _():
        deliver(1).wait_send()

    @pl.when(last_ok)
    def _():
        deliver(2).wait_send()


def solution(mesh):
    nq, nt = mesh.shape["chan"] // 2, mesh.shape["tm"]

    def per_device(traces, live_channels, partners):
        chans, samples = traces.shape
        half = chans // 2
        segs = samples // HOP
        steps = segs // 4
        cols = NFFT // nt
        anywhere = pl.BlockSpec(memory_space=pltpu.HBM)
        by_slot = pl.pallas_call(
            functools.partial(kernel, nq, nt, segs, chans),
            out_shape=jax.ShapeDtypeStruct((LIMIT, chans, cols), F32),
            in_specs=[anywhere] * 7,
            out_specs=pl.BlockSpec(memory_space=pltpu.VMEM),
            scratch_shapes=[
                pltpu.SMEM((1,), jnp.int32),
                pltpu.SMEM((1, LIMIT), jnp.int32),
                pltpu.VMEM((2, HOP), F32),
                pltpu.VMEM((segs, chans, HOP), BF16),
                pltpu.VMEM((5, segs + 1, half, HOP), BF16),
                pltpu.VMEM((5, segs, half, NFFT), BF16),
                pltpu.VMEM((PAIRS, half, NFFT), F32),
                pltpu.VMEM((2, HOP, HOP), BF16),
                pltpu.VMEM((HOP, HOP), BF16),
                pltpu.VMEM((2, HOP, HOP), BF16),
                pltpu.VMEM((nt, PAIRS, half, cols), BF16),
                pltpu.VMEM((nt, PAIRS, half, cols), BF16),
                pltpu.VMEM((PAIRS, half, cols), F32),
                pltpu.VMEM((LIMIT, chans, cols), F32),
                pltpu.SemaphoreType.DMA((segs,)),
                pltpu.SemaphoreType.DMA((6,)),
                pltpu.SemaphoreType.DMA((4, steps)),
                pltpu.SemaphoreType.DMA((5, steps)),
                pltpu.SemaphoreType.DMA((5,)),
                pltpu.SemaphoreType.DMA((5,)),
                pltpu.SemaphoreType.DMA((3, nt)),
                pltpu.SemaphoreType.DMA((3, nt)),
                pltpu.SemaphoreType.DMA((3,)),
                pltpu.SemaphoreType.DMA((3, 2)),
            ],
            compiler_params=pltpu.CompilerParams(
                collective_id=0, has_side_effects=True, vmem_limit_bytes=56 * 1024 * 1024
            ),
        )(
            live_channels,
            partners,
            traces,
            jnp.asarray(taper_rows()),
            jnp.asarray(forward_tables()),
            jnp.asarray(band_table()),
            jnp.asarray(lag_tables(segs * nt)),
        )
        return by_slot.transpose(1, 0, 2)

    in_specs = (P("chan", "tm"), P("chan"), P("chan", None))
    out_specs = P("chan", None, "tm")
    return jax.shard_map(
        per_device, mesh=mesh, in_specs=in_specs, out_specs=out_specs, check_vma=False
    )
```

```python
import functools
import math

import jax
import jax.numpy as jnp
import ml_dtypes
import numpy as np
from jax import lax
from jax.experimental import pallas as pl
from jax.experimental.pallas import tpu as pltpu
from jax.sharding import PartitionSpec as P

NFFT = 1024
HOP = NFFT // 2
SMOOTH = 64
LIMIT = 3
MESH = pl.DeviceIdType.MESH
F32 = jnp.float32
BF16 = jnp.bfloat16

SLOT_A, SLOT_B, SLOT_C, SLOT_D, SLOT_E = range(5)
PAIRS = 8


def bin_order():
    return np.concatenate([np.arange(2, HOP + 1, 2), np.arange(1, HOP, 2)])


def taper_rows():
    steps = np.arange(NFFT, dtype=np.float64)
    return (0.5 - 0.5 * np.cos(steps * (2.0 * math.pi / NFFT))).astype(np.float32).reshape(2, HOP)


def forward_tables():
    samples = np.arange(HOP)[:, None]
    tables = []
    for bins in (bin_order()[None, : HOP // 2], bin_order()[None, HOP // 2 :]):
        phase = (samples * bins % NFFT) * (2.0 * math.pi / NFFT)
        tables.append(np.concatenate([np.cos(phase), -np.sin(phase)], 1))
    return np.stack(tables).astype(ml_dtypes.bfloat16)


def band_table():
    freqs = bin_order() - 1
    start = np.clip(freqs - SMOOTH // 2, 0, HOP - SMOOTH)[None, :]
    source = freqs[:, None]
    return (((source >= start) & (source < start + SMOOTH)) / SMOOTH).astype(ml_dtypes.bfloat16)


def lag_tables(segments):
    shifts = np.arange(HOP)[None, :]
    tables = []
    for bins in (bin_order()[: HOP // 2, None], bin_order()[HOP // 2 :, None]):
        phase = (bins * shifts % NFFT) * (2.0 * math.pi / NFFT)
        weight = np.where(bins < HOP, 2.0, 1.0) / math.sqrt(NFFT) / segments
        tables.append(np.concatenate([weight * np.cos(phase), -weight * np.sin(phase)], 0))
    return np.stack(tables).astype(ml_dtypes.bfloat16)


def chunk_bounds(segs):
    bounds = [(4 * s + 1, 4 * s + 5) for s in range(segs // 4)]
    bounds[0] = (0, 5)
    bounds[-1] = (bounds[-1][0], segs)
    return bounds


def kernel(
    nq, nt, segs, chans,
    live_hbm, partners_hbm, x_ref, taper_hbm, fwd_hbm, band_hbm, lag_hbm, out_ref,
    live, partners, taper, own, buf, white, acc, fwd, band, lagt, part, gath, fin, res,
    load_sem, table_sem, ssem, rsem, hsend, hrecv, asend, arecv, fsend, frecv,
):
    half = chans // 2
    steps = segs // 4
    cols = NFFT // nt
    chunks = chunk_bounds(segs)
    chan = lax.axis_index("chan")
    t = lax.axis_index("tm")
    q = chan // 2
    c = lax.rem(chan, 2)
    below, above = q > 0, q < nq - 1
    corner = jnp.logical_and(q == nq - 2, c == 1)
    from_below = jnp.logical_and(q > 0, q + c < nq)
    incoming = jnp.where(c == 0, q, nq - 1 - q) > 0
    mine = SLOT_B + c
    theirs = SLOT_C - c

    def at(chip, core, time):
        return {"chan": 2 * chip + core, "tm": time}

    for h in range(segs):
        pltpu.make_async_copy(x_ref.at[:, pl.ds(HOP * h, HOP)], own.at[h], load_sem.at[h]).start()
    tables = [
        pltpu.make_async_copy(fwd_hbm, fwd, table_sem.at[0]),
        pltpu.make_async_copy(band_hbm, band, table_sem.at[1]),
        pltpu.make_async_copy(lag_hbm, lagt, table_sem.at[2]),
        pltpu.make_async_copy(taper_hbm, taper, table_sem.at[3]),
        pltpu.make_async_copy(partners_hbm, partners, table_sem.at[4]),
    ]
    live_copy = pltpu.make_async_copy(live_hbm, live, table_sem.at[5])
    live_copy.start()
    for copy in tables:
        copy.start()

    @pl.when(jnp.logical_not(from_below))
    def _():
        buf[SLOT_A] = jnp.zeros((segs + 1, half, HOP), BF16)

    @pl.when(q == nq - 1)
    def _():
        buf[SLOT_D] = jnp.zeros((segs + 1, half, HOP), BF16)

    @pl.when(q >= nq - 2)
    def _():
        res[...] = jnp.zeros(res.shape, F32)

    @pl.when(jnp.logical_not(incoming))
    def _():
        buf[SLOT_E] = jnp.zeros((segs + 1, half, HOP), BF16)

    @pl.when(t == nt - 1)
    def _():
        for slot in range(5):
            buf[slot, segs] = jnp.zeros((half, HOP), BF16)

    barrier = pltpu.get_barrier_semaphore()

    def greet(chip, core, time):
        pl.semaphore_signal(barrier, inc=1, device_id=at(chip, core, time), device_id_type=MESH)

    for d in range(1, nt):
        greet(q, c, lax.rem(t + d, nt))

    def greet_around(time):
        greet(q, 1 - c, time)

        @pl.when(below)
        def _():
            greet(q - 1, 0, time)
            greet(q - 1, 1, time)

        @pl.when(above)
        def _():
            greet(q + 1, 0, time)
            greet(q + 1, 1, time)

    greet_around(t)

    @pl.when(t > 0)
    def _():
        greet_around(t - 1)

    @pl.when(t < nt - 1)
    def _():
        greet_around(t + 1)

    live_copy.wait()
    alive = lax.broadcasted_iota(jnp.int32, (chans, HOP), 0) < live[0]
    mask = jnp.where(alive, F32(1.0), F32(0.0)).astype(BF16)

    def mask_one(h, carry):
        pltpu.make_async_copy(
            x_ref.at[:, pl.ds(pl.multiple_of(HOP * h, HOP), HOP)], own.at[h], load_sem.at[h]
        ).wait()
        own[h] = own[h] * mask
        buf[mine, h] = own[h, pl.ds(pl.multiple_of(half * c, half), half), :]
        return carry

    lax.fori_loop(0, chunks[0][1], mask_one, 0)

    around = 1 + 2 * jnp.where(below, 1, 0) + 2 * jnp.where(above, 1, 0)
    times = 1 + jnp.where(t > 0, 1, 0) + jnp.where(t < nt - 1, 1, 0)
    pl.semaphore_wait(barrier, nt - 1 + around * times)

    outward = 2 * c - 1
    main_ok = (jnp.where(c == 0, q, nq - 1 - q) > 0, jnp.where(c == 0, q, nq - 2 - q) > 0)
    edge_ok = jnp.where(c == 0, nq - 1 - q, q) > 0

    def route(index):
        if index == 0:
            return half * (1 - c), mine, q, 1 - c
        if index in (1, 2):
            return half * (index - 1), 3 * (1 - c), q + outward, index - 1
        if index == 3:
            return half * c, SLOT_E, q - outward, c
        return half * c, mine, q, c

    def stream(index, k):
        lo, hi = chunks[k]
        row, slot, chip, core = route(index)
        return pltpu.make_async_remote_copy(
            src_ref=own.at[pl.ds(lo, hi - lo), pl.ds(row, half), :],
            dst_ref=buf.at[slot, pl.ds(lo, hi - lo)],
            send_sem=ssem.at[index, k],
            recv_sem=rsem.at[slot, k],
            device_id=at(chip, core, t),
            device_id_type=MESH,
        )

    def halo(index):
        row, slot, chip, core = route(index)
        return pltpu.make_async_remote_copy(
            src_ref=own.at[0, pl.ds(row, half), :],
            dst_ref=buf.at[slot, segs],
            send_sem=hsend.at[index],
            recv_sem=hrecv.at[slot],
            device_id=at(chip, core, t - 1),
            device_id_type=MESH,
        )

    def halos(act):
        @pl.when(t > 0)
        def _():
            act(halo(4))
            act(halo(0))

            for n in range(2):
                @pl.when(main_ok[n])
                def _():
                    act(halo(1 + n))

            @pl.when(edge_ok)
            def _():
                act(halo(3))

    def arrive(slot, k):
        lo, hi = chunks[k]
        pltpu.make_async_remote_copy(
            src_ref=own.at[pl.ds(lo, hi - lo), pl.ds(0, half), :],
            dst_ref=buf.at[slot, pl.ds(lo, hi - lo)],
            send_sem=ssem.at[0, k],
            recv_sem=rsem.at[slot, k],
            device_id=at(q, 1 - c, t),
            device_id_type=MESH,
        ).wait_recv()

    def halo_wait(slot):
        @pl.when(t < nt - 1)
        def _():
            pltpu.make_async_remote_copy(
                src_ref=own.at[0, pl.ds(0, half), :],
                dst_ref=buf.at[slot, segs],
                send_sem=hsend.at[0],
                recv_sem=hrecv.at[slot],
                device_id=at(q, c, t + 1),
                device_id_type=MESH,
            ).wait_recv()

    def main_start(k):
        for n in range(2):
            @pl.when(main_ok[n])
            def _():
                stream(1 + n, k).start()

    def main_left(k):
        for n in range(2):
            @pl.when(main_ok[n])
            def _():
                stream(1 + n, k).wait_send()

    def edge_start(k):
        @pl.when(edge_ok)
        def _():
            stream(3, k).start()

    stream(0, 0).start()
    main_start(0)
    halos(lambda copy: copy.start())
    lax.fori_loop(chunks[0][1], segs, mask_one, 0)
    for k in range(1, steps):
        stream(0, k).start()
    main_start(1)

    for copy in tables:
        copy.wait()

    taper_rise, taper_fall = taper[0:1, :], taper[1:2, :]
    quarter = HOP // 2

    def whiten(parts):
        sums, differences = [], []
        for slot, first, count in parts:
            samples = buf[slot, first : first + count + 1].astype(F32)
            rise, fall = samples[:count] * taper_rise, samples[1:] * taper_fall
            sums.append((rise + fall).astype(BF16).reshape(count * half, HOP))
            differences.append((rise - fall).astype(BF16).reshape(count * half, HOP))
        even = jnp.dot(jnp.concatenate(sums, 0), fwd[0], preferred_element_type=F32)
        odd = jnp.dot(jnp.concatenate(differences, 0), fwd[1], preferred_element_type=F32)
        power = [
            (z[:, :quarter] * z[:, :quarter] + z[:, quarter:] * z[:, quarter:]).astype(BF16)
            for z in (even, odd)
        ]
        smooth = jnp.dot(jnp.concatenate(power, 1), band[...], preferred_element_type=F32)
        factor = lax.rsqrt(smooth + 1e-06)
        row = 0
        for slot, first, count in parts:
            rows = slice(row, row + count * half)
            row += count * half
            for n, z in enumerate((even, odd)):
                scale = factor[rows, n * quarter : (n + 1) * quarter]
                for m in range(2):
                    value = (z[rows, m * quarter : (m + 1) * quarter] * scale).astype(BF16)
                    lanes = slice(m * HOP + n * quarter, m * HOP + (n + 1) * quarter)
                    white[slot, first : first + count, :, lanes] = value.reshape(count, half, quarter)

    def cross(pairs, start, count):
        slots = []
        for _, first, second in pairs:
            for slot in (first, second):
                if not any(slot is s for s in slots):
                    slots.append(slot)

        def tile(i, carry):
            rows = pl.ds(pl.multiple_of(16 * (i // 4), 16), 16)
            lanes = pl.multiple_of(128 * lax.rem(i, 4), 128)
            lanes_re, lanes_im = pl.ds(lanes, 128), pl.ds(HOP + lanes, 128)
            sums = [[acc[p, rows, lanes_re], acc[p, rows, lanes_im]] for p, _, _ in pairs]
            for seg in range(start, start + count):
                values = [
                    (
                        white[slot, seg, rows, lanes_re].astype(F32),
                        white[slot, seg, rows, lanes_im].astype(F32),
                    )
                    for slot in slots
                ]
                for n, (_, first, second) in enumerate(pairs):
                    a_re, a_im = [v for s, v in zip(slots, values) if s is first][0]
                    b_re, b_im = [v for s, v in zip(slots, values) if s is second][0]
                    sums[n][0] += a_re * b_re + a_im * b_im
                    sums[n][1] += a_im * b_re - a_re * b_im
            for n, (p, _, _) in enumerate(pairs):
                acc[p, rows, lanes_re] = sums[n][0]
                acc[p, rows, lanes_im] = sums[n][1]
            return carry

        lax.fori_loop(0, (half // 16) * 4, tile, 0)

    def lags_of(first, count):
        stack = acc[first : first + count].reshape(count * half, NFFT)
        high = stack.astype(BF16)
        low = (stack - high.astype(F32)).astype(BF16)
        both = jnp.concatenate([high, low], 0)
        sides = []
        for n in range(2):
            lanes = slice(n * quarter, (n + 1) * quarter)
            lanes_im = slice(HOP + n * quarter, HOP + (n + 1) * quarter)
            side = jnp.dot(
                jnp.concatenate([both[:, lanes], both[:, lanes_im]], 1),
                lagt[n],
                preferred_element_type=F32,
            )
            sides.append(side[: count * half] + side[count * half :])
        even, odd = sides
        lags = jnp.concatenate([(even + odd).astype(BF16), (even - odd).astype(BF16)], 1)
        for time in range(nt):
            part[time, first : first + count] = lags[:, time * cols : (time + 1) * cols].reshape(
                count, half, cols
            )

    def exchange(group, first, count, d):
        peer = lax.rem(t + d, nt)
        return pltpu.make_async_remote_copy(
            src_ref=part.at[peer, pl.ds(first, count)],
            dst_ref=gath.at[t, pl.ds(first, count)],
            send_sem=asend.at[group, d],
            recv_sem=arecv.at[group, t],
            device_id=at(q, c, peer),
            device_id_type=MESH,
        )

    def collect(group, first, count):
        gath[t, first : first + count] = part[t, first : first + count]
        for d in range(1, nt):
            source = lax.rem(t + d, nt)
            pltpu.make_async_remote_copy(
                src_ref=part.at[source, pl.ds(first, count)],
                dst_ref=gath.at[source, pl.ds(first, count)],
                send_sem=asend.at[group, d],
                recv_sem=arecv.at[group, source],
                device_id=at(q, c, source),
                device_id_type=MESH,
            ).wait_recv()
        total = gath[0, first : first + count].astype(F32)
        for time in range(1, nt):
            total += gath[time, first : first + count].astype(F32)
        fin[first : first + count] = total

    def deliver(kind):
        if kind == 0:
            src, dst = fin.at[pl.ds(0, 3)], res.at[pl.ds(0, 3), pl.ds(half * c, half), :]
            device = at(q - 1, 1, t)
        elif kind == 1:
            src, dst = fin.at[pl.ds(3, 2)], res.at[pl.ds(0, 2), pl.ds(half * c, half), :]
            device = at(q, 0, t)
        else:
            src, dst = fin.at[pl.ds(5, 1)], res.at[pl.ds(2, 1), pl.ds(half * c, half), :]
            device = at(jnp.where(c == 0, q - 1, q), 0, t)
        return pltpu.make_async_remote_copy(
            src_ref=src,
            dst_ref=dst,
            send_sem=fsend.at[kind],
            recv_sem=frecv.at[kind, c],
            device_id=device,
            device_id_type=MESH,
        )

    def delivered(kind, core):
        first, count = ((0, 3), (3, 2), (5, 1))[kind]
        pltpu.make_async_remote_copy(
            src_ref=fin.at[pl.ds(first, count)],
            dst_ref=res.at[pl.ds(2 if kind == 2 else 0, count), pl.ds(half * core, half), :],
            send_sem=fsend.at[kind],
            recv_sem=frecv.at[kind, core],
            device_id=at(q, 1 - c, t),
            device_id_type=MESH,
        ).wait_recv()

    acc[...] = jnp.zeros(acc.shape, F32)

    whiten([(mine, 0, 8)])
    arrive(theirs, 0)
    halo_wait(mine)
    whiten([(mine, 8, 8)])
    arrive(theirs, 1)
    whiten([(theirs, 0, 8)])
    cross([(3, SLOT_B, SLOT_C)], 0, 8)
    arrive(theirs, 2)
    arrive(theirs, 3)

    def arrive_sides(k):
        @pl.when(from_below)
        def _():
            arrive(SLOT_A, k)

        @pl.when(above)
        def _():
            arrive(SLOT_D, k)

    halo_wait(theirs)
    whiten([(theirs, 8, 8)])
    cross([(3, SLOT_B, SLOT_C)], 8, 8)

    for k in range(steps):
        main_left(k)
        if k + 2 < steps:
            main_start(k + 2)
        else:
            edge_start(2 * (k + 2 - steps))
            edge_start(2 * (k + 2 - steps) + 1)
        arrive_sides(k)
        if k == steps - 1:
            @pl.when(from_below)
            def _():
                halo_wait(SLOT_A)

            @pl.when(above)
            def _():
                halo_wait(SLOT_D)

        whiten([(SLOT_A, 4 * k, 4), (SLOT_D, 4 * k, 4)])
        cross(
            [(0, SLOT_A, SLOT_B), (1, SLOT_A, SLOT_C), (2, SLOT_A, SLOT_D), (4, SLOT_B, SLOT_D)],
            4 * k,
            4,
        )

    lags_of(0, 5)
    for d in range(1, nt):
        exchange(0, 0, 5, d).start()

    first_white = jnp.where(c == 0, SLOT_E, SLOT_B)
    second_white = jnp.where(c == 0, SLOT_C, SLOT_E)

    for chunks_in, first, count in (((0, 1), 0, 8), ((2,), 8, 4), ((3,), 12, 4)):
        @pl.when(incoming)
        def _():
            for k in chunks_in:
                arrive(SLOT_E, k)
            if first + count == segs:
                halo_wait(SLOT_E)

        whiten([(SLOT_E, first, count)])
        cross([(5, first_white, second_white)], first, count)

    lags_of(5, 1)
    for d in range(1, nt):
        exchange(1, 5, 1, d).start()

    @pl.when(corner)
    def _():
        pairs = [(6, SLOT_C, SLOT_D), (7, SLOT_C, SLOT_E)]
        cross(pairs, 0, 8)
        cross(pairs, 8, 8)
        lags_of(6, 2)
        for d in range(1, nt):
            exchange(2, 6, 2, d).start()

    collect(0, 0, 5)

    @pl.when(from_below)
    def _():
        deliver(0).start()

    @pl.when(c == 1)
    def _():
        deliver(1).start()

    @pl.when(c == 0)
    def _():
        res[0:2, 0:half] = fin[3:5]

    collect(1, 5, 1)
    last_ok = jnp.logical_or(c == 1, from_below)

    @pl.when(last_ok)
    def _():
        deliver(2).start()

    @pl.when(corner)
    def _():
        collect(2, 6, 2)
        res[0:2, half:chans] = fin[6:8]

    @pl.when(c == 0)
    def _():
        delivered(1, 1)
        delivered(2, 1)

        @pl.when(above)
        def _():
            delivered(2, 0)

    @pl.when(jnp.logical_and(c == 1, above))
    def _():
        delivered(0, 0)

    @pl.when(jnp.logical_and(c == 1, q < nq - 2))
    def _():
        delivered(0, 1)

    for slot in range(LIMIT):
        reach = partners[0, slot] - chan
        row = jnp.zeros((chans, cols), F32)
        for offset in range(LIMIT):
            row = jnp.where(reach == offset + 1, res[offset], row)
        out_ref[slot] = row

    for k in range(steps):
        stream(0, k).wait_send()

        @pl.when(edge_ok)
        def _():
            stream(3, k).wait_send()

    halos(lambda copy: copy.wait_send())

    for d in range(1, nt):
        exchange(0, 0, 5, d).wait_send()
        exchange(1, 5, 1, d).wait_send()

    @pl.when(corner)
    def _():
        for d in range(1, nt):
            exchange(2, 6, 2, d).wait_send()

    @pl.when(from_below)
    def _():
        deliver(0).wait_send()

    @pl.when(c == 1)
    def _():
        deliver(1).wait_send()

    @pl.when(last_ok)
    def _():
        deliver(2).wait_send()


def solution(mesh):
    nq, nt = mesh.shape["chan"] // 2, mesh.shape["tm"]

    def per_device(traces, live_channels, partners):
        chans, samples = traces.shape
        half = chans // 2
        segs = samples // HOP
        steps = segs // 4
        cols = NFFT // nt
        anywhere = pl.BlockSpec(memory_space=pltpu.HBM)
        by_slot = pl.pallas_call(
            functools.partial(kernel, nq, nt, segs, chans),
            out_shape=jax.ShapeDtypeStruct((LIMIT, chans, cols), F32),
            in_specs=[anywhere] * 7,
            out_specs=pl.BlockSpec(memory_space=pltpu.VMEM),
            scratch_shapes=[
                pltpu.SMEM((1,), jnp.int32),
                pltpu.SMEM((1, LIMIT), jnp.int32),
                pltpu.VMEM((2, HOP), F32),
                pltpu.VMEM((segs, chans, HOP), BF16),
                pltpu.VMEM((5, segs + 1, half, HOP), BF16),
                pltpu.VMEM((5, segs, half, NFFT), BF16),
                pltpu.VMEM((PAIRS, half, NFFT), F32),
                pltpu.VMEM((2, HOP, HOP), BF16),
                pltpu.VMEM((HOP, HOP), BF16),
                pltpu.VMEM((2, HOP, HOP), BF16),
                pltpu.VMEM((nt, PAIRS, half, cols), BF16),
                pltpu.VMEM((nt, PAIRS, half, cols), BF16),
                pltpu.VMEM((PAIRS, half, cols), F32),
                pltpu.VMEM((LIMIT, chans, cols), F32),
                pltpu.SemaphoreType.DMA((segs,)),
                pltpu.SemaphoreType.DMA((6,)),
                pltpu.SemaphoreType.DMA((4, steps)),
                pltpu.SemaphoreType.DMA((5, steps)),
                pltpu.SemaphoreType.DMA((5,)),
                pltpu.SemaphoreType.DMA((5,)),
                pltpu.SemaphoreType.DMA((3, nt)),
                pltpu.SemaphoreType.DMA((3, nt)),
                pltpu.SemaphoreType.DMA((3,)),
                pltpu.SemaphoreType.DMA((3, 2)),
            ],
            compiler_params=pltpu.CompilerParams(
                collective_id=0, has_side_effects=True, vmem_limit_bytes=56 * 1024 * 1024
            ),
        )(
            live_channels,
            partners,
            traces,
            jnp.asarray(taper_rows()),
            jnp.asarray(forward_tables()),
            jnp.asarray(band_table()),
            jnp.asarray(lag_tables(segs * nt)),
        )
        alive = jnp.arange(chans, dtype=jnp.int32)[:, None, None] < live_channels.reshape(1, 1, 1)
        return jnp.where(alive, by_slot.transpose(1, 0, 2), F32(0.0))

    in_specs = (P("chan", "tm"), P("chan"), P("chan", None))
    out_specs = P("chan", None, "tm")
    return jax.shard_map(
        per_device, mesh=mesh, in_specs=in_specs, out_specs=out_specs, check_vma=False
    )
```

```python
import functools
import math

import jax
import jax.numpy as jnp
import ml_dtypes
import numpy as np
from jax import lax
from jax.experimental import pallas as pl
from jax.experimental.pallas import tpu as pltpu
from jax.sharding import PartitionSpec as P

NFFT = 1024
HOP = NFFT // 2
SMOOTH = 64
LIMIT = 3
MESH = pl.DeviceIdType.MESH
F32 = jnp.float32
BF16 = jnp.bfloat16

SLOT_A, SLOT_B, SLOT_C, SLOT_D, SLOT_E = range(5)
PAIRS = 8


def bin_order():
    return np.concatenate([np.arange(2, HOP + 1, 2), np.arange(1, HOP, 2)])


def taper_rows():
    steps = np.arange(NFFT, dtype=np.float64)
    return (0.5 - 0.5 * np.cos(steps * (2.0 * math.pi / NFFT))).astype(np.float32).reshape(2, HOP)


def forward_tables():
    samples = np.arange(HOP)[:, None]
    tables = []
    for bins in (bin_order()[None, : HOP // 2], bin_order()[None, HOP // 2 :]):
        phase = (samples * bins % NFFT) * (2.0 * math.pi / NFFT)
        tables.append(np.concatenate([np.cos(phase), -np.sin(phase)], 1))
    return np.stack(tables).astype(ml_dtypes.bfloat16)


def band_table():
    freqs = bin_order() - 1
    start = np.clip(freqs - SMOOTH // 2, 0, HOP - SMOOTH)[None, :]
    source = freqs[:, None]
    return (((source >= start) & (source < start + SMOOTH)) / SMOOTH).astype(ml_dtypes.bfloat16)


def lag_tables(segments):
    shifts = np.arange(HOP)[None, :]
    tables = []
    for bins in (bin_order()[: HOP // 2, None], bin_order()[HOP // 2 :, None]):
        phase = (bins * shifts % NFFT) * (2.0 * math.pi / NFFT)
        weight = np.where(bins < HOP, 2.0, 1.0) / math.sqrt(NFFT) / segments
        tables.append(np.concatenate([weight * np.cos(phase), -weight * np.sin(phase)], 0))
    return np.stack(tables).astype(ml_dtypes.bfloat16)


def chunk_bounds(segs):
    bounds = [(4 * s + 1, 4 * s + 5) for s in range(segs // 4)]
    bounds[0] = (0, 5)
    bounds[-1] = (bounds[-1][0], segs)
    return bounds


def kernel(
    nq, nt, segs, chans,
    live_hbm, partners_hbm, x_ref, taper_hbm, fwd_hbm, band_hbm, lag_hbm, out_ref,
    live, partners, taper, own, buf, white, acc, fwd, band, lagt, part, gath, fin, res,
    load_sem, table_sem, ssem, rsem, hsend, hrecv, asend, arecv, fsend, frecv,
):
    half = chans // 2
    steps = segs // 4
    cols = NFFT // nt
    chunks = chunk_bounds(segs)
    chan = lax.axis_index("chan")
    t = lax.axis_index("tm")
    q = chan // 2
    c = lax.rem(chan, 2)
    below, above = q > 0, q < nq - 1
    corner = jnp.logical_and(q == nq - 2, c == 1)
    from_below = jnp.logical_and(q > 0, q + c < nq)
    incoming = jnp.where(c == 0, q, nq - 1 - q) > 0
    mine = SLOT_B + c
    theirs = SLOT_C - c

    def at(chip, core, time):
        return {"chan": 2 * chip + core, "tm": time}

    def load(h):
        pltpu.make_async_copy(x_ref.at[:, pl.ds(HOP * h, HOP)], own.at[h], load_sem.at[h]).start()

    live_copy = pltpu.make_async_copy(live_hbm, live, table_sem.at[5])
    live_copy.start()
    for h in range(chunks[0][1]):
        load(h)

    @pl.when(q >= nq - 2)
    def _():
        res[...] = jnp.zeros(res.shape, F32)

    barrier = pltpu.get_barrier_semaphore()

    def greet(chip, core, time):
        pl.semaphore_signal(barrier, inc=1, device_id=at(chip, core, time), device_id_type=MESH)

    for d in range(1, nt):
        greet(q, c, lax.rem(t + d, nt))

    def greet_around(time):
        greet(q, 1 - c, time)

        @pl.when(below)
        def _():
            greet(q - 1, 0, time)
            greet(q - 1, 1, time)

        @pl.when(above)
        def _():
            greet(q + 1, 0, time)
            greet(q + 1, 1, time)

    greet_around(t)

    @pl.when(t > 0)
    def _():
        greet_around(t - 1)

    @pl.when(t < nt - 1)
    def _():
        greet_around(t + 1)

    for h in range(chunks[0][1], segs):
        load(h)

    tables = [
        pltpu.make_async_copy(fwd_hbm, fwd, table_sem.at[0]),
        pltpu.make_async_copy(band_hbm, band, table_sem.at[1]),
        pltpu.make_async_copy(lag_hbm, lagt, table_sem.at[2]),
        pltpu.make_async_copy(taper_hbm, taper, table_sem.at[3]),
        pltpu.make_async_copy(partners_hbm, partners, table_sem.at[4]),
    ]
    for copy in tables:
        copy.start()

    @pl.when(jnp.logical_not(from_below))
    def _():
        buf[SLOT_A] = jnp.zeros((segs + 1, half, HOP), BF16)

    @pl.when(q == nq - 1)
    def _():
        buf[SLOT_D] = jnp.zeros((segs + 1, half, HOP), BF16)

    @pl.when(jnp.logical_not(incoming))
    def _():
        buf[SLOT_E] = jnp.zeros((segs + 1, half, HOP), BF16)

    @pl.when(t == nt - 1)
    def _():
        for slot in range(5):
            buf[slot, segs] = jnp.zeros((half, HOP), BF16)

    live_copy.wait()
    alive = lax.broadcasted_iota(jnp.int32, (chans, HOP), 0) < live[0]
    mask = jnp.where(alive, F32(1.0), F32(0.0)).astype(BF16)

    def mask_one(h, carry):
        pltpu.make_async_copy(
            x_ref.at[:, pl.ds(pl.multiple_of(HOP * h, HOP), HOP)], own.at[h], load_sem.at[h]
        ).wait()
        own[h] = own[h] * mask
        buf[mine, h] = own[h, pl.ds(pl.multiple_of(half * c, half), half), :]
        return carry

    lax.fori_loop(0, chunks[0][1], mask_one, 0)

    around = 1 + 2 * jnp.where(below, 1, 0) + 2 * jnp.where(above, 1, 0)
    times = 1 + jnp.where(t > 0, 1, 0) + jnp.where(t < nt - 1, 1, 0)
    pl.semaphore_wait(barrier, nt - 1 + around * times)

    outward = 2 * c - 1
    main_ok = (jnp.where(c == 0, q, nq - 1 - q) > 0, jnp.where(c == 0, q, nq - 2 - q) > 0)
    edge_ok = jnp.where(c == 0, nq - 1 - q, q) > 0

    def route(index):
        if index == 0:
            return half * (1 - c), mine, q, 1 - c
        if index in (1, 2):
            return half * (index - 1), 3 * (1 - c), q + outward, index - 1
        if index == 3:
            return half * c, SLOT_E, q - outward, c
        return half * c, mine, q, c

    def stream(index, k):
        lo, hi = chunks[k]
        row, slot, chip, core = route(index)
        return pltpu.make_async_remote_copy(
            src_ref=own.at[pl.ds(lo, hi - lo), pl.ds(row, half), :],
            dst_ref=buf.at[slot, pl.ds(lo, hi - lo)],
            send_sem=ssem.at[index, k],
            recv_sem=rsem.at[slot, k],
            device_id=at(chip, core, t),
            device_id_type=MESH,
        )

    def halo(index):
        row, slot, chip, core = route(index)
        return pltpu.make_async_remote_copy(
            src_ref=own.at[0, pl.ds(row, half), :],
            dst_ref=buf.at[slot, segs],
            send_sem=hsend.at[index],
            recv_sem=hrecv.at[slot],
            device_id=at(chip, core, t - 1),
            device_id_type=MESH,
        )

    def halos(act):
        @pl.when(t > 0)
        def _():
            act(halo(4))
            act(halo(0))

            for n in range(2):
                @pl.when(main_ok[n])
                def _():
                    act(halo(1 + n))

            @pl.when(edge_ok)
            def _():
                act(halo(3))

    def arrive(slot, k):
        lo, hi = chunks[k]
        pltpu.make_async_remote_copy(
            src_ref=own.at[pl.ds(lo, hi - lo), pl.ds(0, half), :],
            dst_ref=buf.at[slot, pl.ds(lo, hi - lo)],
            send_sem=ssem.at[0, k],
            recv_sem=rsem.at[slot, k],
            device_id=at(q, 1 - c, t),
            device_id_type=MESH,
        ).wait_recv()

    def halo_wait(slot):
        @pl.when(t < nt - 1)
        def _():
            pltpu.make_async_remote_copy(
                src_ref=own.at[0, pl.ds(0, half), :],
                dst_ref=buf.at[slot, segs],
                send_sem=hsend.at[0],
                recv_sem=hrecv.at[slot],
                device_id=at(q, c, t + 1),
                device_id_type=MESH,
            ).wait_recv()

    def main_start(k):
        for n in range(2):
            @pl.when(main_ok[n])
            def _():
                stream(1 + n, k).start()

    def main_left(k):
        for n in range(2):
            @pl.when(main_ok[n])
            def _():
                stream(1 + n, k).wait_send()

    def edge_start(k):
        @pl.when(edge_ok)
        def _():
            stream(3, k).start()

    stream(0, 0).start()
    main_start(0)
    halos(lambda copy: copy.start())
    lax.fori_loop(chunks[0][1], segs, mask_one, 0)
    for k in range(1, steps):
        stream(0, k).start()
    main_start(1)

    for copy in tables:
        copy.wait()

    taper_rise, taper_fall = taper[0:1, :], taper[1:2, :]
    quarter = HOP // 2

    def whiten(parts):
        sums, differences = [], []
        for slot, first, count in parts:
            samples = buf[slot, first : first + count + 1].astype(F32)
            rise, fall = samples[:count] * taper_rise, samples[1:] * taper_fall
            sums.append((rise + fall).astype(BF16).reshape(count * half, HOP))
            differences.append((rise - fall).astype(BF16).reshape(count * half, HOP))
        even = jnp.dot(jnp.concatenate(sums, 0), fwd[0], preferred_element_type=F32)
        odd = jnp.dot(jnp.concatenate(differences, 0), fwd[1], preferred_element_type=F32)
        power = [
            (z[:, :quarter] * z[:, :quarter] + z[:, quarter:] * z[:, quarter:]).astype(BF16)
            for z in (even, odd)
        ]
        smooth = jnp.dot(jnp.concatenate(power, 1), band[...], preferred_element_type=F32)
        factor = lax.rsqrt(smooth + 1e-06)
        row = 0
        for slot, first, count in parts:
            rows = slice(row, row + count * half)
            row += count * half
            for n, z in enumerate((even, odd)):
                scale = factor[rows, n * quarter : (n + 1) * quarter]
                for m in range(2):
                    value = (z[rows, m * quarter : (m + 1) * quarter] * scale).astype(BF16)
                    lanes = slice(m * HOP + n * quarter, m * HOP + (n + 1) * quarter)
                    white[slot, first : first + count, :, lanes] = value.reshape(count, half, quarter)

    def cross(pairs, start, count):
        slots = []
        for _, first, second in pairs:
            for slot in (first, second):
                if not any(slot is s for s in slots):
                    slots.append(slot)

        def tile(i, carry):
            rows = pl.ds(pl.multiple_of(16 * (i // 4), 16), 16)
            lanes = pl.multiple_of(128 * lax.rem(i, 4), 128)
            lanes_re, lanes_im = pl.ds(lanes, 128), pl.ds(HOP + lanes, 128)
            sums = [[acc[p, rows, lanes_re], acc[p, rows, lanes_im]] for p, _, _ in pairs]
            for seg in range(start, start + count):
                values = [
                    (
                        white[slot, seg, rows, lanes_re].astype(F32),
                        white[slot, seg, rows, lanes_im].astype(F32),
                    )
                    for slot in slots
                ]
                for n, (_, first, second) in enumerate(pairs):
                    a_re, a_im = [v for s, v in zip(slots, values) if s is first][0]
                    b_re, b_im = [v for s, v in zip(slots, values) if s is second][0]
                    sums[n][0] += a_re * b_re + a_im * b_im
                    sums[n][1] += a_im * b_re - a_re * b_im
            for n, (p, _, _) in enumerate(pairs):
                acc[p, rows, lanes_re] = sums[n][0]
                acc[p, rows, lanes_im] = sums[n][1]
            return carry

        lax.fori_loop(0, (half // 16) * 4, tile, 0)

    def lags_of(first, count):
        stack = acc[first : first + count].reshape(count * half, NFFT)
        high = stack.astype(BF16)
        low = (stack - high.astype(F32)).astype(BF16)
        both = jnp.concatenate([high, low], 0)
        sides = []
        for n in range(2):
            lanes = slice(n * quarter, (n + 1) * quarter)
            lanes_im = slice(HOP + n * quarter, HOP + (n + 1) * quarter)
            side = jnp.dot(
                jnp.concatenate([both[:, lanes], both[:, lanes_im]], 1),
                lagt[n],
                preferred_element_type=F32,
            )
            sides.append(side[: count * half] + side[count * half :])
        even, odd = sides
        lags = jnp.concatenate([(even + odd).astype(BF16), (even - odd).astype(BF16)], 1)
        for time in range(nt):
            part[time, first : first + count] = lags[:, time * cols : (time + 1) * cols].reshape(
                count, half, cols
            )

    def exchange(group, first, count, d):
        peer = lax.rem(t + d, nt)
        return pltpu.make_async_remote_copy(
            src_ref=part.at[peer, pl.ds(first, count)],
            dst_ref=gath.at[t, pl.ds(first, count)],
            send_sem=asend.at[group, d],
            recv_sem=arecv.at[group, t],
            device_id=at(q, c, peer),
            device_id_type=MESH,
        )

    def collect(group, first, count):
        gath[t, first : first + count] = part[t, first : first + count]
        for d in range(1, nt):
            source = lax.rem(t + d, nt)
            pltpu.make_async_remote_copy(
                src_ref=part.at[source, pl.ds(first, count)],
                dst_ref=gath.at[source, pl.ds(first, count)],
                send_sem=asend.at[group, d],
                recv_sem=arecv.at[group, source],
                device_id=at(q, c, source),
                device_id_type=MESH,
            ).wait_recv()
        total = gath[0, first : first + count].astype(F32)
        for time in range(1, nt):
            total += gath[time, first : first + count].astype(F32)
        fin[first : first + count] = total

    def deliver(kind):
        if kind == 0:
            src, dst = fin.at[pl.ds(0, 3)], res.at[pl.ds(0, 3), pl.ds(half * c, half), :]
            device = at(q - 1, 1, t)
        elif kind == 1:
            src, dst = fin.at[pl.ds(3, 2)], res.at[pl.ds(0, 2), pl.ds(half * c, half), :]
            device = at(q, 0, t)
        else:
            src, dst = fin.at[pl.ds(5, 1)], res.at[pl.ds(2, 1), pl.ds(half * c, half), :]
            device = at(jnp.where(c == 0, q - 1, q), 0, t)
        return pltpu.make_async_remote_copy(
            src_ref=src,
            dst_ref=dst,
            send_sem=fsend.at[kind],
            recv_sem=frecv.at[kind, c],
            device_id=device,
            device_id_type=MESH,
        )

    def delivered(kind, core):
        first, count = ((0, 3), (3, 2), (5, 1))[kind]
        pltpu.make_async_remote_copy(
            src_ref=fin.at[pl.ds(first, count)],
            dst_ref=res.at[pl.ds(2 if kind == 2 else 0, count), pl.ds(half * core, half), :],
            send_sem=fsend.at[kind],
            recv_sem=frecv.at[kind, core],
            device_id=at(q, 1 - c, t),
            device_id_type=MESH,
        ).wait_recv()

    acc[...] = jnp.zeros(acc.shape, F32)

    whiten([(mine, 0, 8)])
    arrive(theirs, 0)
    halo_wait(mine)
    whiten([(mine, 8, 8)])
    arrive(theirs, 1)
    whiten([(theirs, 0, 8)])
    cross([(3, SLOT_B, SLOT_C)], 0, 8)
    arrive(theirs, 2)
    arrive(theirs, 3)

    def arrive_sides(k):
        @pl.when(from_below)
        def _():
            arrive(SLOT_A, k)

        @pl.when(above)
        def _():
            arrive(SLOT_D, k)

    halo_wait(theirs)
    whiten([(theirs, 8, 8)])
    cross([(3, SLOT_B, SLOT_C)], 8, 8)

    for k in range(steps):
        main_left(k)
        if k + 2 < steps:
            main_start(k + 2)
        else:
            edge_start(2 * (k + 2 - steps))
            edge_start(2 * (k + 2 - steps) + 1)
        arrive_sides(k)
        if k == steps - 1:
            @pl.when(from_below)
            def _():
                halo_wait(SLOT_A)

            @pl.when(above)
            def _():
                halo_wait(SLOT_D)

        whiten([(SLOT_A, 4 * k, 4), (SLOT_D, 4 * k, 4)])
        cross(
            [(0, SLOT_A, SLOT_B), (1, SLOT_A, SLOT_C), (2, SLOT_A, SLOT_D), (4, SLOT_B, SLOT_D)],
            4 * k,
            4,
        )

    lags_of(0, 5)
    for d in range(1, nt):
        exchange(0, 0, 5, d).start()

    first_white = jnp.where(c == 0, SLOT_E, SLOT_B)
    second_white = jnp.where(c == 0, SLOT_C, SLOT_E)

    for chunks_in, first, count in (((0, 1), 0, 8), ((2,), 8, 4), ((3,), 12, 4)):
        @pl.when(incoming)
        def _():
            for k in chunks_in:
                arrive(SLOT_E, k)
            if first + count == segs:
                halo_wait(SLOT_E)

        whiten([(SLOT_E, first, count)])
        cross([(5, first_white, second_white)], first, count)

    lags_of(5, 1)
    for d in range(1, nt):
        exchange(1, 5, 1, d).start()

    @pl.when(corner)
    def _():
        pairs = [(6, SLOT_C, SLOT_D), (7, SLOT_C, SLOT_E)]
        cross(pairs, 0, 8)
        cross(pairs, 8, 8)
        lags_of(6, 2)
        for d in range(1, nt):
            exchange(2, 6, 2, d).start()

    collect(0, 0, 5)

    @pl.when(from_below)
    def _():
        deliver(0).start()

    @pl.when(c == 1)
    def _():
        deliver(1).start()

    @pl.when(c == 0)
    def _():
        res[0:2, 0:half] = fin[3:5]

    collect(1, 5, 1)
    last_ok = jnp.logical_or(c == 1, from_below)

    @pl.when(last_ok)
    def _():
        deliver(2).start()

    @pl.when(corner)
    def _():
        collect(2, 6, 2)
        res[0:2, half:chans] = fin[6:8]

    @pl.when(c == 0)
    def _():
        delivered(1, 1)
        delivered(2, 1)

        @pl.when(above)
        def _():
            delivered(2, 0)

    @pl.when(jnp.logical_and(c == 1, above))
    def _():
        delivered(0, 0)

    @pl.when(jnp.logical_and(c == 1, q < nq - 2))
    def _():
        delivered(0, 1)

    for slot in range(LIMIT):
        reach = partners[0, slot] - chan
        row = jnp.zeros((chans, cols), F32)
        for offset in range(LIMIT):
            row = jnp.where(reach == offset + 1, res[offset], row)
        out_ref[slot] = row

    for k in range(steps):
        stream(0, k).wait_send()

        @pl.when(edge_ok)
        def _():
            stream(3, k).wait_send()

    halos(lambda copy: copy.wait_send())

    for d in range(1, nt):
        exchange(0, 0, 5, d).wait_send()
        exchange(1, 5, 1, d).wait_send()

    @pl.when(corner)
    def _():
        for d in range(1, nt):
            exchange(2, 6, 2, d).wait_send()

    @pl.when(from_below)
    def _():
        deliver(0).wait_send()

    @pl.when(c == 1)
    def _():
        deliver(1).wait_send()

    @pl.when(last_ok)
    def _():
        deliver(2).wait_send()


def solution(mesh):
    nq, nt = mesh.shape["chan"] // 2, mesh.shape["tm"]

    def per_device(traces, live_channels, partners):
        chans, samples = traces.shape
        half = chans // 2
        segs = samples // HOP
        steps = segs // 4
        cols = NFFT // nt
        anywhere = pl.BlockSpec(memory_space=pltpu.HBM)
        by_slot = pl.pallas_call(
            functools.partial(kernel, nq, nt, segs, chans),
            out_shape=jax.ShapeDtypeStruct((LIMIT, chans, cols), F32),
            in_specs=[anywhere] * 7,
            out_specs=pl.BlockSpec(memory_space=pltpu.VMEM),
            scratch_shapes=[
                pltpu.SMEM((1,), jnp.int32),
                pltpu.SMEM((1, LIMIT), jnp.int32),
                pltpu.VMEM((2, HOP), F32),
                pltpu.VMEM((segs, chans, HOP), BF16),
                pltpu.VMEM((5, segs + 1, half, HOP), BF16),
                pltpu.VMEM((5, segs, half, NFFT), BF16),
                pltpu.VMEM((PAIRS, half, NFFT), F32),
                pltpu.VMEM((2, HOP, HOP), BF16),
                pltpu.VMEM((HOP, HOP), BF16),
                pltpu.VMEM((2, HOP, HOP), BF16),
                pltpu.VMEM((nt, PAIRS, half, cols), BF16),
                pltpu.VMEM((nt, PAIRS, half, cols), BF16),
                pltpu.VMEM((PAIRS, half, cols), F32),
                pltpu.VMEM((LIMIT, chans, cols), F32),
                pltpu.SemaphoreType.DMA((segs,)),
                pltpu.SemaphoreType.DMA((6,)),
                pltpu.SemaphoreType.DMA((4, steps)),
                pltpu.SemaphoreType.DMA((5, steps)),
                pltpu.SemaphoreType.DMA((5,)),
                pltpu.SemaphoreType.DMA((5,)),
                pltpu.SemaphoreType.DMA((3, nt)),
                pltpu.SemaphoreType.DMA((3, nt)),
                pltpu.SemaphoreType.DMA((3,)),
                pltpu.SemaphoreType.DMA((3, 2)),
            ],
            compiler_params=pltpu.CompilerParams(
                collective_id=0, has_side_effects=True, vmem_limit_bytes=56 * 1024 * 1024
            ),
        )(
            live_channels,
            partners,
            traces,
            jnp.asarray(taper_rows()),
            jnp.asarray(forward_tables()),
            jnp.asarray(band_table()),
            jnp.asarray(lag_tables(segs * nt)),
        )
        return by_slot.transpose(1, 0, 2)

    in_specs = (P("chan", "tm"), P("chan"), P("chan", None))
    out_specs = P("chan", None, "tm")
    return jax.shard_map(
        per_device, mesh=mesh, in_specs=in_specs, out_specs=out_specs, check_vma=False
    )
```

```python
import functools
import math

import jax
import jax.numpy as jnp
import ml_dtypes
import numpy as np
from jax import lax
from jax.experimental import pallas as pl
from jax.experimental.pallas import tpu as pltpu
from jax.sharding import PartitionSpec as P

NFFT = 1024
HOP = NFFT // 2
SMOOTH = 64
LIMIT = 3
MESH = pl.DeviceIdType.MESH
F32 = jnp.float32
BF16 = jnp.bfloat16

SLOT_A, SLOT_B, SLOT_C, SLOT_D, SLOT_E = range(5)
PAIRS = 8


def bin_order():
    return np.concatenate([np.arange(2, HOP + 1, 2), np.arange(1, HOP, 2)])


def taper_rows():
    steps = np.arange(NFFT, dtype=np.float64)
    return (0.5 - 0.5 * np.cos(steps * (2.0 * math.pi / NFFT))).astype(np.float32).reshape(2, HOP)


def forward_tables():
    samples = np.arange(HOP)[:, None]
    tables = []
    for bins in (bin_order()[None, : HOP // 2], bin_order()[None, HOP // 2 :]):
        phase = (samples * bins % NFFT) * (2.0 * math.pi / NFFT)
        tables.append(np.concatenate([np.cos(phase), -np.sin(phase)], 1))
    return np.stack(tables).astype(ml_dtypes.bfloat16)


def band_table():
    freqs = bin_order() - 1
    start = np.clip(freqs - SMOOTH // 2, 0, HOP - SMOOTH)[None, :]
    source = freqs[:, None]
    return (((source >= start) & (source < start + SMOOTH)) / SMOOTH).astype(ml_dtypes.bfloat16)


def lag_tables(segments):
    shifts = np.arange(HOP)[None, :]
    tables = []
    for bins in (bin_order()[: HOP // 2, None], bin_order()[HOP // 2 :, None]):
        phase = (bins * shifts % NFFT) * (2.0 * math.pi / NFFT)
        weight = np.where(bins < HOP, 2.0, 1.0) / math.sqrt(NFFT) / segments
        tables.append(np.concatenate([weight * np.cos(phase), -weight * np.sin(phase)], 0))
    return np.stack(tables).astype(ml_dtypes.bfloat16)


def chunk_bounds(segs):
    bounds = [(4 * s + 1, 4 * s + 5) for s in range(segs // 4)]
    bounds[0] = (0, 5)
    bounds[-1] = (bounds[-1][0], segs)
    return bounds


def kernel(
    nq, nt, segs, chans,
    live_hbm, partners_hbm, x_ref, taper_hbm, fwd_hbm, band_hbm, lag_hbm, out_ref,
    live, partners, taper, own, buf, white, acc, fwd, band, lagt, part, gath, fin, res,
    load_sem, table_sem, ssem, rsem, hsend, hrecv, asend, arecv, fsend, frecv,
):
    half = chans // 2
    steps = segs // 4
    cols = NFFT // nt
    chunks = chunk_bounds(segs)
    chan = lax.axis_index("chan")
    t = lax.axis_index("tm")
    q = chan // 2
    c = lax.rem(chan, 2)
    below, above = q > 0, q < nq - 1
    corner = jnp.logical_and(q == nq - 2, c == 1)
    from_below = jnp.logical_and(q > 0, q + c < nq)
    incoming = jnp.where(c == 0, q, nq - 1 - q) > 0
    mine = SLOT_B + c
    theirs = SLOT_C - c

    def at(chip, core, time):
        return {"chan": 2 * chip + core, "tm": time}

    def load(h):
        pltpu.make_async_copy(x_ref.at[:, pl.ds(HOP * h, HOP)], own.at[h], load_sem.at[h]).start()

    live_copy = pltpu.make_async_copy(live_hbm, live, table_sem.at[5])
    live_copy.start()
    for h in range(chunks[0][1]):
        load(h)

    @pl.when(q >= nq - 2)
    def _():
        res[...] = jnp.zeros(res.shape, F32)

    barrier = pltpu.get_barrier_semaphore()

    def greet(chip, core, time):
        pl.semaphore_signal(barrier, inc=1, device_id=at(chip, core, time), device_id_type=MESH)

    for d in range(1, nt):
        greet(q, c, lax.rem(t + d, nt))

    def greet_around(time):
        greet(q, 1 - c, time)

        @pl.when(below)
        def _():
            greet(q - 1, 0, time)
            greet(q - 1, 1, time)

        @pl.when(above)
        def _():
            greet(q + 1, 0, time)
            greet(q + 1, 1, time)

    greet_around(t)

    @pl.when(t > 0)
    def _():
        greet_around(t - 1)

    @pl.when(t < nt - 1)
    def _():
        greet_around(t + 1)

    for h in range(chunks[0][1], segs):
        load(h)

    tables = [
        pltpu.make_async_copy(fwd_hbm, fwd, table_sem.at[0]),
        pltpu.make_async_copy(band_hbm, band, table_sem.at[1]),
        pltpu.make_async_copy(lag_hbm, lagt, table_sem.at[2]),
        pltpu.make_async_copy(taper_hbm, taper, table_sem.at[3]),
        pltpu.make_async_copy(partners_hbm, partners, table_sem.at[4]),
    ]
    for copy in tables:
        copy.start()

    @pl.when(jnp.logical_not(from_below))
    def _():
        buf[SLOT_A] = jnp.zeros((segs + 1, half, HOP), BF16)

    @pl.when(q == nq - 1)
    def _():
        buf[SLOT_D] = jnp.zeros((segs + 1, half, HOP), BF16)

    @pl.when(jnp.logical_not(incoming))
    def _():
        buf[SLOT_E] = jnp.zeros((segs + 1, half, HOP), BF16)

    @pl.when(t == nt - 1)
    def _():
        for slot in range(5):
            buf[slot, segs] = jnp.zeros((half, HOP), BF16)

    live_copy.wait()
    alive = lax.broadcasted_iota(jnp.int32, (chans, HOP), 0) < live[0]
    mask = jnp.where(alive, F32(1.0), F32(0.0)).astype(BF16)

    def mask_one(h, carry):
        pltpu.make_async_copy(
            x_ref.at[:, pl.ds(pl.multiple_of(HOP * h, HOP), HOP)], own.at[h], load_sem.at[h]
        ).wait()
        own[h] = own[h] * mask
        buf[mine, h] = own[h, pl.ds(pl.multiple_of(half * c, half), half), :]
        return carry

    lax.fori_loop(0, chunks[0][1], mask_one, 0)

    around = 1 + 2 * jnp.where(below, 1, 0) + 2 * jnp.where(above, 1, 0)
    times = 1 + jnp.where(t > 0, 1, 0) + jnp.where(t < nt - 1, 1, 0)
    pl.semaphore_wait(barrier, nt - 1 + around * times)

    outward = 2 * c - 1
    main_ok = (jnp.where(c == 0, q, nq - 1 - q) > 0, jnp.where(c == 0, q, nq - 2 - q) > 0)
    edge_ok = jnp.where(c == 0, nq - 1 - q, q) > 0

    def route(index):
        if index == 0:
            return half * (1 - c), mine, q, 1 - c
        if index in (1, 2):
            return half * (index - 1), 3 * (1 - c), q + outward, index - 1
        if index == 3:
            return half * c, SLOT_E, q - outward, c
        return half * c, mine, q, c

    def stream(index, k):
        lo, hi = chunks[k]
        row, slot, chip, core = route(index)
        return pltpu.make_async_remote_copy(
            src_ref=own.at[pl.ds(lo, hi - lo), pl.ds(row, half), :],
            dst_ref=buf.at[slot, pl.ds(lo, hi - lo)],
            send_sem=ssem.at[index, k],
            recv_sem=rsem.at[slot, k],
            device_id=at(chip, core, t),
            device_id_type=MESH,
        )

    def halo(index):
        row, slot, chip, core = route(index)
        return pltpu.make_async_remote_copy(
            src_ref=own.at[0, pl.ds(row, half), :],
            dst_ref=buf.at[slot, segs],
            send_sem=hsend.at[index],
            recv_sem=hrecv.at[slot],
            device_id=at(chip, core, t - 1),
            device_id_type=MESH,
        )

    def halos(act):
        @pl.when(t > 0)
        def _():
            act(halo(4))
            act(halo(0))

            for n in range(2):
                @pl.when(main_ok[n])
                def _():
                    act(halo(1 + n))

            @pl.when(edge_ok)
            def _():
                act(halo(3))

    def arrive(slot, k):
        lo, hi = chunks[k]
        pltpu.make_async_remote_copy(
            src_ref=own.at[pl.ds(lo, hi - lo), pl.ds(0, half), :],
            dst_ref=buf.at[slot, pl.ds(lo, hi - lo)],
            send_sem=ssem.at[0, k],
            recv_sem=rsem.at[slot, k],
            device_id=at(q, 1 - c, t),
            device_id_type=MESH,
        ).wait_recv()

    def halo_wait(slot):
        @pl.when(t < nt - 1)
        def _():
            pltpu.make_async_remote_copy(
                src_ref=own.at[0, pl.ds(0, half), :],
                dst_ref=buf.at[slot, segs],
                send_sem=hsend.at[0],
                recv_sem=hrecv.at[slot],
                device_id=at(q, c, t + 1),
                device_id_type=MESH,
            ).wait_recv()

    def main_start(k):
        for n in range(2):
            @pl.when(main_ok[n])
            def _():
                stream(1 + n, k).start()

    def main_left(k):
        for n in range(2):
            @pl.when(main_ok[n])
            def _():
                stream(1 + n, k).wait_send()

    def edge_start(k):
        @pl.when(edge_ok)
        def _():
            stream(3, k).start()

    stream(0, 0).start()
    main_start(0)
    halos(lambda copy: copy.start())
    lax.fori_loop(chunks[0][1], segs, mask_one, 0)
    for k in range(1, steps):
        stream(0, k).start()
    main_start(1)

    for copy in tables:
        copy.wait()

    taper_rise, taper_fall = taper[0:1, :], taper[1:2, :]
    quarter = HOP // 2

    def whiten(parts):
        sums, differences = [], []
        for slot, first, count in parts:
            samples = buf[slot, first : first + count + 1].astype(F32)
            rise, fall = samples[:count] * taper_rise, samples[1:] * taper_fall
            sums.append((rise + fall).astype(BF16).reshape(count * half, HOP))
            differences.append((rise - fall).astype(BF16).reshape(count * half, HOP))
        even = jnp.dot(jnp.concatenate(sums, 0), fwd[0], preferred_element_type=F32)
        odd = jnp.dot(jnp.concatenate(differences, 0), fwd[1], preferred_element_type=F32)
        power = [
            (z[:, :quarter] * z[:, :quarter] + z[:, quarter:] * z[:, quarter:]).astype(BF16)
            for z in (even, odd)
        ]
        smooth = jnp.dot(jnp.concatenate(power, 1), band[...], preferred_element_type=F32)
        factor = lax.rsqrt(smooth + 1e-06)
        row = 0
        for slot, first, count in parts:
            rows = slice(row, row + count * half)
            row += count * half
            for n, z in enumerate((even, odd)):
                scale = factor[rows, n * quarter : (n + 1) * quarter]
                for m in range(2):
                    value = (z[rows, m * quarter : (m + 1) * quarter] * scale).astype(BF16)
                    lanes = slice(m * HOP + n * quarter, m * HOP + (n + 1) * quarter)
                    white[slot, first : first + count, :, lanes] = value.reshape(count, half, quarter)

    def cross(pairs, start, count):
        slots = []
        for _, first, second in pairs:
            for slot in (first, second):
                if not any(slot is s for s in slots):
                    slots.append(slot)

        def tile(i, carry):
            rows = pl.ds(pl.multiple_of(16 * (i // 4), 16), 16)
            lanes = pl.multiple_of(128 * lax.rem(i, 4), 128)
            lanes_re, lanes_im = pl.ds(lanes, 128), pl.ds(HOP + lanes, 128)
            sums = [[acc[p, rows, lanes_re], acc[p, rows, lanes_im]] for p, _, _ in pairs]
            for seg in range(start, start + count):
                values = [
                    (
                        white[slot, seg, rows, lanes_re].astype(F32),
                        white[slot, seg, rows, lanes_im].astype(F32),
                    )
                    for slot in slots
                ]
                for n, (_, first, second) in enumerate(pairs):
                    a_re, a_im = [v for s, v in zip(slots, values) if s is first][0]
                    b_re, b_im = [v for s, v in zip(slots, values) if s is second][0]
                    sums[n][0] += a_re * b_re + a_im * b_im
                    sums[n][1] += a_im * b_re - a_re * b_im
            for n, (p, _, _) in enumerate(pairs):
                acc[p, rows, lanes_re] = sums[n][0]
                acc[p, rows, lanes_im] = sums[n][1]
            return carry

        lax.fori_loop(0, (half // 16) * 4, tile, 0)

    def lags_of(first, count):
        stack = acc[first : first + count].reshape(count * half, NFFT)
        high = stack.astype(BF16)
        low = (stack - high.astype(F32)).astype(BF16)
        both = jnp.concatenate([high, low], 0)
        sides = []
        for n in range(2):
            lanes = slice(n * quarter, (n + 1) * quarter)
            lanes_im = slice(HOP + n * quarter, HOP + (n + 1) * quarter)
            side = jnp.dot(
                jnp.concatenate([both[:, lanes], both[:, lanes_im]], 1),
                lagt[n],
                preferred_element_type=F32,
            )
            sides.append(side[: count * half] + side[count * half :])
        even, odd = sides
        lags = jnp.concatenate([(even + odd).astype(BF16), (even - odd).astype(BF16)], 1)
        for time in range(nt):
            part[time, first : first + count] = lags[:, time * cols : (time + 1) * cols].reshape(
                count, half, cols
            )

    farthest = sorted(range(1, nt), key=lambda d: -min(d, nt - d))

    def exchange(group, first, count, d):
        peer = lax.rem(t + d, nt)
        return pltpu.make_async_remote_copy(
            src_ref=part.at[peer, pl.ds(first, count)],
            dst_ref=gath.at[t, pl.ds(first, count)],
            send_sem=asend.at[group, d],
            recv_sem=arecv.at[group, t],
            device_id=at(q, c, peer),
            device_id_type=MESH,
        )

    def collect(group, first, count):
        gath[t, first : first + count] = part[t, first : first + count]
        for d in range(1, nt):
            source = lax.rem(t + d, nt)
            pltpu.make_async_remote_copy(
                src_ref=part.at[source, pl.ds(first, count)],
                dst_ref=gath.at[source, pl.ds(first, count)],
                send_sem=asend.at[group, d],
                recv_sem=arecv.at[group, source],
                device_id=at(q, c, source),
                device_id_type=MESH,
            ).wait_recv()
        total = gath[0, first : first + count].astype(F32)
        for time in range(1, nt):
            total += gath[time, first : first + count].astype(F32)
        fin[first : first + count] = total

    def deliver(kind):
        if kind == 0:
            src, dst = fin.at[pl.ds(0, 3)], res.at[pl.ds(0, 3), pl.ds(half * c, half), :]
            device = at(q - 1, 1, t)
        elif kind == 1:
            src, dst = fin.at[pl.ds(3, 2)], res.at[pl.ds(0, 2), pl.ds(half * c, half), :]
            device = at(q, 0, t)
        else:
            src, dst = fin.at[pl.ds(5, 1)], res.at[pl.ds(2, 1), pl.ds(half * c, half), :]
            device = at(jnp.where(c == 0, q - 1, q), 0, t)
        return pltpu.make_async_remote_copy(
            src_ref=src,
            dst_ref=dst,
            send_sem=fsend.at[kind],
            recv_sem=frecv.at[kind, c],
            device_id=device,
            device_id_type=MESH,
        )

    def delivered(kind, core):
        first, count = ((0, 3), (3, 2), (5, 1))[kind]
        pltpu.make_async_remote_copy(
            src_ref=fin.at[pl.ds(first, count)],
            dst_ref=res.at[pl.ds(2 if kind == 2 else 0, count), pl.ds(half * core, half), :],
            send_sem=fsend.at[kind],
            recv_sem=frecv.at[kind, core],
            device_id=at(q, 1 - c, t),
            device_id_type=MESH,
        ).wait_recv()

    acc[...] = jnp.zeros(acc.shape, F32)

    whiten([(mine, 0, 8)])
    arrive(theirs, 0)
    halo_wait(mine)
    whiten([(mine, 8, 8)])
    arrive(theirs, 1)
    whiten([(theirs, 0, 8)])
    cross([(3, SLOT_B, SLOT_C)], 0, 8)
    arrive(theirs, 2)
    arrive(theirs, 3)

    def arrive_sides(k):
        @pl.when(from_below)
        def _():
            arrive(SLOT_A, k)

        @pl.when(above)
        def _():
            arrive(SLOT_D, k)

    halo_wait(theirs)
    whiten([(theirs, 8, 8)])
    cross([(3, SLOT_B, SLOT_C)], 8, 8)

    for k in range(steps):
        main_left(k)
        if k + 2 < steps:
            main_start(k + 2)
        else:
            edge_start(2 * (k + 2 - steps))
            edge_start(2 * (k + 2 - steps) + 1)
        arrive_sides(k)
        if k == steps - 1:
            @pl.when(from_below)
            def _():
                halo_wait(SLOT_A)

            @pl.when(above)
            def _():
                halo_wait(SLOT_D)

        whiten([(SLOT_A, 4 * k, 4), (SLOT_D, 4 * k, 4)])
        cross(
            [(0, SLOT_A, SLOT_B), (1, SLOT_A, SLOT_C), (2, SLOT_A, SLOT_D), (4, SLOT_B, SLOT_D)],
            4 * k,
            4,
        )

    lags_of(0, 5)
    for d in farthest:
        exchange(0, 0, 5, d).start()

    first_white = jnp.where(c == 0, SLOT_E, SLOT_B)
    second_white = jnp.where(c == 0, SLOT_C, SLOT_E)

    for chunks_in, first, count in (((0, 1), 0, 8), ((2,), 8, 4), ((3,), 12, 4)):
        @pl.when(incoming)
        def _():
            for k in chunks_in:
                arrive(SLOT_E, k)
            if first + count == segs:
                halo_wait(SLOT_E)

        whiten([(SLOT_E, first, count)])
        cross([(5, first_white, second_white)], first, count)

    lags_of(5, 1)
    for d in farthest:
        exchange(1, 5, 1, d).start()

    @pl.when(corner)
    def _():
        pairs = [(6, SLOT_C, SLOT_D), (7, SLOT_C, SLOT_E)]
        cross(pairs, 0, 8)
        cross(pairs, 8, 8)
        lags_of(6, 2)
        for d in range(1, nt):
            exchange(2, 6, 2, d).start()

    collect(0, 0, 5)

    @pl.when(from_below)
    def _():
        deliver(0).start()

    @pl.when(c == 1)
    def _():
        deliver(1).start()

    @pl.when(c == 0)
    def _():
        res[0:2, 0:half] = fin[3:5]

    collect(1, 5, 1)
    last_ok = jnp.logical_or(c == 1, from_below)

    @pl.when(last_ok)
    def _():
        deliver(2).start()

    @pl.when(corner)
    def _():
        collect(2, 6, 2)
        res[0:2, half:chans] = fin[6:8]

    @pl.when(c == 0)
    def _():
        delivered(1, 1)
        delivered(2, 1)

        @pl.when(above)
        def _():
            delivered(2, 0)

    @pl.when(jnp.logical_and(c == 1, above))
    def _():
        delivered(0, 0)

    @pl.when(jnp.logical_and(c == 1, q < nq - 2))
    def _():
        delivered(0, 1)

    for slot in range(LIMIT):
        reach = partners[0, slot] - chan
        row = jnp.zeros((chans, cols), F32)
        for offset in range(LIMIT):
            row = jnp.where(reach == offset + 1, res[offset], row)
        out_ref[slot] = row

    for k in range(steps):
        stream(0, k).wait_send()

        @pl.when(edge_ok)
        def _():
            stream(3, k).wait_send()

    halos(lambda copy: copy.wait_send())

    for d in range(1, nt):
        exchange(0, 0, 5, d).wait_send()
        exchange(1, 5, 1, d).wait_send()

    @pl.when(corner)
    def _():
        for d in range(1, nt):
            exchange(2, 6, 2, d).wait_send()

    @pl.when(from_below)
    def _():
        deliver(0).wait_send()

    @pl.when(c == 1)
    def _():
        deliver(1).wait_send()

    @pl.when(last_ok)
    def _():
        deliver(2).wait_send()


def solution(mesh):
    nq, nt = mesh.shape["chan"] // 2, mesh.shape["tm"]

    def per_device(traces, live_channels, partners):
        chans, samples = traces.shape
        half = chans // 2
        segs = samples // HOP
        steps = segs // 4
        cols = NFFT // nt
        anywhere = pl.BlockSpec(memory_space=pltpu.HBM)
        by_slot = pl.pallas_call(
            functools.partial(kernel, nq, nt, segs, chans),
            out_shape=jax.ShapeDtypeStruct((LIMIT, chans, cols), F32),
            in_specs=[anywhere] * 7,
            out_specs=pl.BlockSpec(memory_space=pltpu.VMEM),
            scratch_shapes=[
                pltpu.SMEM((1,), jnp.int32),
                pltpu.SMEM((1, LIMIT), jnp.int32),
                pltpu.VMEM((2, HOP), F32),
                pltpu.VMEM((segs, chans, HOP), BF16),
                pltpu.VMEM((5, segs + 1, half, HOP), BF16),
                pltpu.VMEM((5, segs, half, NFFT), BF16),
                pltpu.VMEM((PAIRS, half, NFFT), F32),
                pltpu.VMEM((2, HOP, HOP), BF16),
                pltpu.VMEM((HOP, HOP), BF16),
                pltpu.VMEM((2, HOP, HOP), BF16),
                pltpu.VMEM((nt, PAIRS, half, cols), BF16),
                pltpu.VMEM((nt, PAIRS, half, cols), BF16),
                pltpu.VMEM((PAIRS, half, cols), F32),
                pltpu.VMEM((LIMIT, chans, cols), F32),
                pltpu.SemaphoreType.DMA((segs,)),
                pltpu.SemaphoreType.DMA((6,)),
                pltpu.SemaphoreType.DMA((4, steps)),
                pltpu.SemaphoreType.DMA((5, steps)),
                pltpu.SemaphoreType.DMA((5,)),
                pltpu.SemaphoreType.DMA((5,)),
                pltpu.SemaphoreType.DMA((3, nt)),
                pltpu.SemaphoreType.DMA((3, nt)),
                pltpu.SemaphoreType.DMA((3,)),
                pltpu.SemaphoreType.DMA((3, 2)),
            ],
            compiler_params=pltpu.CompilerParams(
                collective_id=0, has_side_effects=True, vmem_limit_bytes=56 * 1024 * 1024
            ),
        )(
            live_channels,
            partners,
            traces,
            jnp.asarray(taper_rows()),
            jnp.asarray(forward_tables()),
            jnp.asarray(band_table()),
            jnp.asarray(lag_tables(segs * nt)),
        )
        return by_slot.transpose(1, 0, 2)

    in_specs = (P("chan", "tm"), P("chan"), P("chan", None))
    out_specs = P("chan", None, "tm")
    return jax.shard_map(
        per_device, mesh=mesh, in_specs=in_specs, out_specs=out_specs, check_vma=False
    )
```

```python
import functools
import math

import jax
import jax.numpy as jnp
import ml_dtypes
import numpy as np
from jax import lax
from jax.experimental import pallas as pl
from jax.experimental.pallas import tpu as pltpu
from jax.sharding import PartitionSpec as P

NFFT = 1024
HOP = NFFT // 2
SMOOTH = 64
LIMIT = 3
MESH = pl.DeviceIdType.MESH
F32 = jnp.float32
BF16 = jnp.bfloat16

SLOT_A, SLOT_B, SLOT_C, SLOT_D, SLOT_E = range(5)
PAIRS = 8


def bin_order():
    return np.concatenate([np.arange(2, HOP + 1, 2), np.arange(1, HOP, 2)])


def taper_rows():
    steps = np.arange(NFFT, dtype=np.float64)
    return (0.5 - 0.5 * np.cos(steps * (2.0 * math.pi / NFFT))).astype(np.float32).reshape(2, HOP)


def forward_tables():
    samples = np.arange(HOP)[:, None]
    tables = []
    for bins in (bin_order()[None, : HOP // 2], bin_order()[None, HOP // 2 :]):
        phase = (samples * bins % NFFT) * (2.0 * math.pi / NFFT)
        tables.append(np.concatenate([np.cos(phase), -np.sin(phase)], 1))
    return np.stack(tables).astype(ml_dtypes.bfloat16)


def band_table():
    freqs = bin_order() - 1
    start = np.clip(freqs - SMOOTH // 2, 0, HOP - SMOOTH)[None, :]
    source = freqs[:, None]
    return (((source >= start) & (source < start + SMOOTH)) / SMOOTH).astype(ml_dtypes.bfloat16)


def lag_tables(segments):
    shifts = np.arange(HOP)[None, :]
    tables = []
    for bins in (bin_order()[: HOP // 2, None], bin_order()[HOP // 2 :, None]):
        phase = (bins * shifts % NFFT) * (2.0 * math.pi / NFFT)
        weight = np.where(bins < HOP, 2.0, 1.0) / math.sqrt(NFFT) / segments
        tables.append(np.concatenate([weight * np.cos(phase), -weight * np.sin(phase)], 0))
    return np.stack(tables).astype(ml_dtypes.bfloat16)


def chunk_bounds(segs):
    bounds = [(4 * s + 1, 4 * s + 5) for s in range(segs // 4)]
    bounds[0] = (0, 5)
    bounds[-1] = (bounds[-1][0], segs)
    return bounds


def kernel(
    nq, nt, segs, chans,
    live_hbm, partners_hbm, x_ref, taper_hbm, fwd_hbm, band_hbm, lag_hbm, out_ref,
    live, partners, taper, own, buf, white, acc, fwd, band, lagt, part, gath, fin, res,
    load_sem, table_sem, ssem, rsem, hsend, hrecv, asend, arecv, fsend, frecv,
):
    half = chans // 2
    steps = segs // 4
    cols = NFFT // nt
    chunks = chunk_bounds(segs)
    chan = lax.axis_index("chan")
    t = lax.axis_index("tm")
    q = chan // 2
    c = lax.rem(chan, 2)
    below, above = q > 0, q < nq - 1
    corner = jnp.logical_and(q == nq - 2, c == 1)
    from_below = jnp.logical_and(q > 0, q + c < nq)
    incoming = jnp.where(c == 0, q, nq - 1 - q) > 0
    mine = SLOT_B + c
    theirs = SLOT_C - c

    def at(chip, core, time):
        return {"chan": 2 * chip + core, "tm": time}

    def load(h):
        pltpu.make_async_copy(x_ref.at[:, pl.ds(HOP * h, HOP)], own.at[h], load_sem.at[h]).start()

    live_copy = pltpu.make_async_copy(live_hbm, live, table_sem.at[5])
    live_copy.start()
    for h in range(chunks[0][1]):
        load(h)

    @pl.when(q >= nq - 2)
    def _():
        res[...] = jnp.zeros(res.shape, F32)

    barrier = pltpu.get_barrier_semaphore()

    def greet(chip, core, time):
        pl.semaphore_signal(barrier, inc=1, device_id=at(chip, core, time), device_id_type=MESH)

    for d in range(1, nt):
        greet(q, c, lax.rem(t + d, nt))

    def greet_around(time):
        greet(q, 1 - c, time)

        @pl.when(below)
        def _():
            greet(q - 1, 0, time)
            greet(q - 1, 1, time)

        @pl.when(above)
        def _():
            greet(q + 1, 0, time)
            greet(q + 1, 1, time)

    greet_around(t)

    @pl.when(t > 0)
    def _():
        greet_around(t - 1)

    @pl.when(t < nt - 1)
    def _():
        greet_around(t + 1)

    for h in range(chunks[0][1], segs):
        load(h)

    tables = [
        pltpu.make_async_copy(fwd_hbm, fwd, table_sem.at[0]),
        pltpu.make_async_copy(band_hbm, band, table_sem.at[1]),
        pltpu.make_async_copy(lag_hbm, lagt, table_sem.at[2]),
        pltpu.make_async_copy(taper_hbm, taper, table_sem.at[3]),
        pltpu.make_async_copy(partners_hbm, partners, table_sem.at[4]),
    ]
    for copy in tables:
        copy.start()

    @pl.when(jnp.logical_not(from_below))
    def _():
        buf[SLOT_A] = jnp.zeros((segs + 1, half, HOP), BF16)

    @pl.when(q == nq - 1)
    def _():
        buf[SLOT_D] = jnp.zeros((segs + 1, half, HOP), BF16)

    @pl.when(jnp.logical_not(incoming))
    def _():
        buf[SLOT_E] = jnp.zeros((segs + 1, half, HOP), BF16)

    @pl.when(t == nt - 1)
    def _():
        for slot in range(5):
            buf[slot, segs] = jnp.zeros((half, HOP), BF16)

    live_copy.wait()
    alive = lax.broadcasted_iota(jnp.int32, (chans, HOP), 0) < live[0]
    mask = jnp.where(alive, F32(1.0), F32(0.0)).astype(BF16)

    def mask_one(h, carry):
        pltpu.make_async_copy(
            x_ref.at[:, pl.ds(pl.multiple_of(HOP * h, HOP), HOP)], own.at[h], load_sem.at[h]
        ).wait()
        own[h] = own[h] * mask
        buf[mine, h] = own[h, pl.ds(pl.multiple_of(half * c, half), half), :]
        return carry

    lax.fori_loop(0, chunks[0][1], mask_one, 0)

    around = 1 + 2 * jnp.where(below, 1, 0) + 2 * jnp.where(above, 1, 0)
    times = 1 + jnp.where(t > 0, 1, 0) + jnp.where(t < nt - 1, 1, 0)
    pl.semaphore_wait(barrier, nt - 1 + around * times)

    outward = 2 * c - 1
    main_ok = (jnp.where(c == 0, q, nq - 1 - q) > 0, jnp.where(c == 0, q, nq - 2 - q) > 0)
    edge_ok = jnp.where(c == 0, nq - 1 - q, q) > 0

    def route(index):
        if index == 0:
            return half * (1 - c), mine, q, 1 - c
        if index in (1, 2):
            return half * (index - 1), 3 * (1 - c), q + outward, index - 1
        if index == 3:
            return half * c, SLOT_E, q - outward, c
        return half * c, mine, q, c

    def stream(index, k):
        lo, hi = chunks[k]
        row, slot, chip, core = route(index)
        return pltpu.make_async_remote_copy(
            src_ref=own.at[pl.ds(lo, hi - lo), pl.ds(row, half), :],
            dst_ref=buf.at[slot, pl.ds(lo, hi - lo)],
            send_sem=ssem.at[index, k],
            recv_sem=rsem.at[slot, k],
            device_id=at(chip, core, t),
            device_id_type=MESH,
        )

    def halo(index):
        row, slot, chip, core = route(index)
        return pltpu.make_async_remote_copy(
            src_ref=own.at[0, pl.ds(row, half), :],
            dst_ref=buf.at[slot, segs],
            send_sem=hsend.at[index],
            recv_sem=hrecv.at[slot],
            device_id=at(chip, core, t - 1),
            device_id_type=MESH,
        )

    def halos(act):
        @pl.when(t > 0)
        def _():
            act(halo(4))
            act(halo(0))

            for n in range(2):
                @pl.when(main_ok[n])
                def _():
                    act(halo(1 + n))

            @pl.when(edge_ok)
            def _():
                act(halo(3))

    def arrive(slot, k):
        lo, hi = chunks[k]
        pltpu.make_async_remote_copy(
            src_ref=own.at[pl.ds(lo, hi - lo), pl.ds(0, half), :],
            dst_ref=buf.at[slot, pl.ds(lo, hi - lo)],
            send_sem=ssem.at[0, k],
            recv_sem=rsem.at[slot, k],
            device_id=at(q, 1 - c, t),
            device_id_type=MESH,
        ).wait_recv()

    def halo_wait(slot):
        @pl.when(t < nt - 1)
        def _():
            pltpu.make_async_remote_copy(
                src_ref=own.at[0, pl.ds(0, half), :],
                dst_ref=buf.at[slot, segs],
                send_sem=hsend.at[0],
                recv_sem=hrecv.at[slot],
                device_id=at(q, c, t + 1),
                device_id_type=MESH,
            ).wait_recv()

    def main_start(k):
        for n in range(2):
            @pl.when(main_ok[n])
            def _():
                stream(1 + n, k).start()

    def main_left(k):
        for n in range(2):
            @pl.when(main_ok[n])
            def _():
                stream(1 + n, k).wait_send()

    def edge_start(k):
        @pl.when(edge_ok)
        def _():
            stream(3, k).start()

    stream(0, 0).start()
    main_start(0)
    halos(lambda copy: copy.start())
    lax.fori_loop(chunks[0][1], segs, mask_one, 0)
    for k in range(1, steps):
        stream(0, k).start()
    main_start(1)

    for copy in tables:
        copy.wait()

    taper_rise, taper_fall = taper[0:1, :], taper[1:2, :]
    quarter = HOP // 2

    def whiten(parts):
        sums, differences = [], []
        for slot, first, count in parts:
            samples = buf[slot, first : first + count + 1].astype(F32)
            rise, fall = samples[:count] * taper_rise, samples[1:] * taper_fall
            sums.append((rise + fall).astype(BF16).reshape(count * half, HOP))
            differences.append((rise - fall).astype(BF16).reshape(count * half, HOP))
        even = jnp.dot(jnp.concatenate(sums, 0), fwd[0], preferred_element_type=F32)
        odd = jnp.dot(jnp.concatenate(differences, 0), fwd[1], preferred_element_type=F32)
        power = [
            (z[:, :quarter] * z[:, :quarter] + z[:, quarter:] * z[:, quarter:]).astype(BF16)
            for z in (even, odd)
        ]
        smooth = jnp.dot(jnp.concatenate(power, 1), band[...], preferred_element_type=F32)
        factor = lax.rsqrt(smooth + 1e-06)
        row = 0
        for slot, first, count in parts:
            rows = slice(row, row + count * half)
            row += count * half
            for n, z in enumerate((even, odd)):
                scale = factor[rows, n * quarter : (n + 1) * quarter]
                for m in range(2):
                    value = (z[rows, m * quarter : (m + 1) * quarter] * scale).astype(BF16)
                    lanes = slice(m * HOP + n * quarter, m * HOP + (n + 1) * quarter)
                    white[slot, first : first + count, :, lanes] = value.reshape(count, half, quarter)

    def cross(pairs, start, count):
        slots = []
        for _, first, second in pairs:
            for slot in (first, second):
                if not any(slot is s for s in slots):
                    slots.append(slot)

        def tile(i, carry):
            rows = pl.ds(pl.multiple_of(16 * (i // 4), 16), 16)
            lanes = pl.multiple_of(128 * lax.rem(i, 4), 128)
            lanes_re, lanes_im = pl.ds(lanes, 128), pl.ds(HOP + lanes, 128)
            sums = [[acc[p, rows, lanes_re], acc[p, rows, lanes_im]] for p, _, _ in pairs]
            for seg in range(start, start + count):
                values = [
                    (
                        white[slot, seg, rows, lanes_re].astype(F32),
                        white[slot, seg, rows, lanes_im].astype(F32),
                    )
                    for slot in slots
                ]
                for n, (_, first, second) in enumerate(pairs):
                    a_re, a_im = [v for s, v in zip(slots, values) if s is first][0]
                    b_re, b_im = [v for s, v in zip(slots, values) if s is second][0]
                    sums[n][0] += a_re * b_re + a_im * b_im
                    sums[n][1] += a_im * b_re - a_re * b_im
            for n, (p, _, _) in enumerate(pairs):
                acc[p, rows, lanes_re] = sums[n][0]
                acc[p, rows, lanes_im] = sums[n][1]
            return carry

        lax.fori_loop(0, (half // 16) * 4, tile, 0)

    def lags_of(first, count):
        stack = acc[first : first + count].reshape(count * half, NFFT)
        high = stack.astype(BF16)
        low = (stack - high.astype(F32)).astype(BF16)
        both = jnp.concatenate([high, low], 0)
        sides = []
        for n in range(2):
            lanes = slice(n * quarter, (n + 1) * quarter)
            lanes_im = slice(HOP + n * quarter, HOP + (n + 1) * quarter)
            side = jnp.dot(
                jnp.concatenate([both[:, lanes], both[:, lanes_im]], 1),
                lagt[n],
                preferred_element_type=F32,
            )
            sides.append(side[: count * half] + side[count * half :])
        even, odd = sides
        lags = jnp.concatenate([(even + odd).astype(BF16), (even - odd).astype(BF16)], 1)
        for time in range(nt):
            part[time, first : first + count] = lags[:, time * cols : (time + 1) * cols].reshape(
                count, half, cols
            )

    def exchange(group, first, count, d):
        peer = lax.rem(t + d, nt)
        return pltpu.make_async_remote_copy(
            src_ref=part.at[peer, pl.ds(first, count)],
            dst_ref=gath.at[t, pl.ds(first, count)],
            send_sem=asend.at[group, d],
            recv_sem=arecv.at[group, t],
            device_id=at(q, c, peer),
            device_id_type=MESH,
        )

    def collect(group, first, count):
        gath[t, first : first + count] = part[t, first : first + count]
        for d in range(1, nt):
            source = lax.rem(t + d, nt)
            pltpu.make_async_remote_copy(
                src_ref=part.at[source, pl.ds(first, count)],
                dst_ref=gath.at[source, pl.ds(first, count)],
                send_sem=asend.at[group, d],
                recv_sem=arecv.at[group, source],
                device_id=at(q, c, source),
                device_id_type=MESH,
            ).wait_recv()
        total = gath[0, first : first + count].astype(F32)
        for time in range(1, nt):
            total += gath[time, first : first + count].astype(F32)
        fin[first : first + count] = total

    def deliver(kind):
        if kind == 0:
            src, dst = fin.at[pl.ds(0, 3)], res.at[pl.ds(0, 3), pl.ds(half * c, half), :]
            device = at(q - 1, 1, t)
        elif kind == 1:
            src, dst = fin.at[pl.ds(3, 2)], res.at[pl.ds(0, 2), pl.ds(half * c, half), :]
            device = at(q, 0, t)
        else:
            src, dst = fin.at[pl.ds(5, 1)], res.at[pl.ds(2, 1), pl.ds(half * c, half), :]
            device = at(jnp.where(c == 0, q - 1, q), 0, t)
        return pltpu.make_async_remote_copy(
            src_ref=src,
            dst_ref=dst,
            send_sem=fsend.at[kind],
            recv_sem=frecv.at[kind, c],
            device_id=device,
            device_id_type=MESH,
        )

    def delivered(kind, core):
        first, count = ((0, 3), (3, 2), (5, 1))[kind]
        pltpu.make_async_remote_copy(
            src_ref=fin.at[pl.ds(first, count)],
            dst_ref=res.at[pl.ds(2 if kind == 2 else 0, count), pl.ds(half * core, half), :],
            send_sem=fsend.at[kind],
            recv_sem=frecv.at[kind, core],
            device_id=at(q, 1 - c, t),
            device_id_type=MESH,
        ).wait_recv()

    acc[...] = jnp.zeros(acc.shape, F32)

    whiten([(mine, 0, 8)])
    arrive(theirs, 0)
    halo_wait(mine)
    whiten([(mine, 8, 8)])
    arrive(theirs, 1)
    whiten([(theirs, 0, 8)])
    cross([(3, SLOT_B, SLOT_C)], 0, 8)
    arrive(theirs, 2)
    arrive(theirs, 3)

    def arrive_sides(k):
        @pl.when(from_below)
        def _():
            arrive(SLOT_A, k)

        @pl.when(above)
        def _():
            arrive(SLOT_D, k)

    main_left(0)
    main_start(2)
    halo_wait(theirs)
    whiten([(theirs, 8, 8)])
    cross([(3, SLOT_B, SLOT_C)], 8, 8)

    for k in range(steps):
        if k > 0:
            main_left(k)
        if 0 < k < steps - 2:
            main_start(k + 2)
        if k >= steps - 2:
            edge_start(2 * (k + 2 - steps))
            edge_start(2 * (k + 2 - steps) + 1)
        arrive_sides(k)
        if k == steps - 1:
            @pl.when(from_below)
            def _():
                halo_wait(SLOT_A)

            @pl.when(above)
            def _():
                halo_wait(SLOT_D)

        whiten([(SLOT_A, 4 * k, 4), (SLOT_D, 4 * k, 4)])
        cross(
            [(0, SLOT_A, SLOT_B), (1, SLOT_A, SLOT_C), (2, SLOT_A, SLOT_D), (4, SLOT_B, SLOT_D)],
            4 * k,
            4,
        )

    lags_of(0, 5)
    for d in range(1, nt):
        exchange(0, 0, 5, d).start()

    first_white = jnp.where(c == 0, SLOT_E, SLOT_B)
    second_white = jnp.where(c == 0, SLOT_C, SLOT_E)

    for chunks_in, first, count in (((0, 1), 0, 8), ((2,), 8, 4), ((3,), 12, 4)):
        @pl.when(incoming)
        def _():
            for k in chunks_in:
                arrive(SLOT_E, k)
            if first + count == segs:
                halo_wait(SLOT_E)

        whiten([(SLOT_E, first, count)])
        cross([(5, first_white, second_white)], first, count)

    lags_of(5, 1)
    for d in range(1, nt):
        exchange(1, 5, 1, d).start()

    @pl.when(corner)
    def _():
        pairs = [(6, SLOT_C, SLOT_D), (7, SLOT_C, SLOT_E)]
        cross(pairs, 0, 8)
        cross(pairs, 8, 8)
        lags_of(6, 2)
        for d in range(1, nt):
            exchange(2, 6, 2, d).start()

    collect(0, 0, 5)

    @pl.when(from_below)
    def _():
        deliver(0).start()

    @pl.when(c == 1)
    def _():
        deliver(1).start()

    @pl.when(c == 0)
    def _():
        res[0:2, 0:half] = fin[3:5]

    collect(1, 5, 1)
    last_ok = jnp.logical_or(c == 1, from_below)

    @pl.when(last_ok)
    def _():
        deliver(2).start()

    @pl.when(corner)
    def _():
        collect(2, 6, 2)
        res[0:2, half:chans] = fin[6:8]

    @pl.when(c == 0)
    def _():
        delivered(1, 1)
        delivered(2, 1)

        @pl.when(above)
        def _():
            delivered(2, 0)

    @pl.when(jnp.logical_and(c == 1, above))
    def _():
        delivered(0, 0)

    @pl.when(jnp.logical_and(c == 1, q < nq - 2))
    def _():
        delivered(0, 1)

    for slot in range(LIMIT):
        reach = partners[0, slot] - chan
        row = jnp.zeros((chans, cols), F32)
        for offset in range(LIMIT):
            row = jnp.where(reach == offset + 1, res[offset], row)
        out_ref[slot] = row

    for k in range(steps):
        stream(0, k).wait_send()

        @pl.when(edge_ok)
        def _():
            stream(3, k).wait_send()

    halos(lambda copy: copy.wait_send())

    for d in range(1, nt):
        exchange(0, 0, 5, d).wait_send()
        exchange(1, 5, 1, d).wait_send()

    @pl.when(corner)
    def _():
        for d in range(1, nt):
            exchange(2, 6, 2, d).wait_send()

    @pl.when(from_below)
    def _():
        deliver(0).wait_send()

    @pl.when(c == 1)
    def _():
        deliver(1).wait_send()

    @pl.when(last_ok)
    def _():
        deliver(2).wait_send()


def solution(mesh):
    nq, nt = mesh.shape["chan"] // 2, mesh.shape["tm"]

    def per_device(traces, live_channels, partners):
        chans, samples = traces.shape
        half = chans // 2
        segs = samples // HOP
        steps = segs // 4
        cols = NFFT // nt
        anywhere = pl.BlockSpec(memory_space=pltpu.HBM)
        by_slot = pl.pallas_call(
            functools.partial(kernel, nq, nt, segs, chans),
            out_shape=jax.ShapeDtypeStruct((LIMIT, chans, cols), F32),
            in_specs=[anywhere] * 7,
            out_specs=pl.BlockSpec(memory_space=pltpu.VMEM),
            scratch_shapes=[
                pltpu.SMEM((1,), jnp.int32),
                pltpu.SMEM((1, LIMIT), jnp.int32),
                pltpu.VMEM((2, HOP), F32),
                pltpu.VMEM((segs, chans, HOP), BF16),
                pltpu.VMEM((5, segs + 1, half, HOP), BF16),
                pltpu.VMEM((5, segs, half, NFFT), BF16),
                pltpu.VMEM((PAIRS, half, NFFT), F32),
                pltpu.VMEM((2, HOP, HOP), BF16),
                pltpu.VMEM((HOP, HOP), BF16),
                pltpu.VMEM((2, HOP, HOP), BF16),
                pltpu.VMEM((nt, PAIRS, half, cols), BF16),
                pltpu.VMEM((nt, PAIRS, half, cols), BF16),
                pltpu.VMEM((PAIRS, half, cols), F32),
                pltpu.VMEM((LIMIT, chans, cols), F32),
                pltpu.SemaphoreType.DMA((segs,)),
                pltpu.SemaphoreType.DMA((6,)),
                pltpu.SemaphoreType.DMA((4, steps)),
                pltpu.SemaphoreType.DMA((5, steps)),
                pltpu.SemaphoreType.DMA((5,)),
                pltpu.SemaphoreType.DMA((5,)),
                pltpu.SemaphoreType.DMA((3, nt)),
                pltpu.SemaphoreType.DMA((3, nt)),
                pltpu.SemaphoreType.DMA((3,)),
                pltpu.SemaphoreType.DMA((3, 2)),
            ],
            compiler_params=pltpu.CompilerParams(
                collective_id=0, has_side_effects=True, vmem_limit_bytes=56 * 1024 * 1024
            ),
        )(
            live_channels,
            partners,
            traces,
            jnp.asarray(taper_rows()),
            jnp.asarray(forward_tables()),
            jnp.asarray(band_table()),
            jnp.asarray(lag_tables(segs * nt)),
        )
        return by_slot.transpose(1, 0, 2)

    in_specs = (P("chan", "tm"), P("chan"), P("chan", None))
    out_specs = P("chan", None, "tm")
    return jax.shard_map(
        per_device, mesh=mesh, in_specs=in_specs, out_specs=out_specs, check_vma=False
    )
```
